512 devices in a mesh: grp: 16 (over z), shard: 32 (over x, y, core).
Axes of the slice: x: 4, y: 4, z: 16, core: 2. Of those that a mesh axis runs over, the one named last changes fastest.
Arguments:
- owner_shard: int32 [2, 65536, 16, 1], P(None, ('grp', 'shard')), may hold values from 0 to 31; in each aligned block of 2048 rows (0 to 2047, 2048 to 4095, ..., all dimensions but the last counted through in order) at most 128 rows name the same one
- local_row: int32 [2, 65536, 16], P(None, ('grp', 'shard')), may hold values from 0 to 511
- click_label: int32 [2, 65536], P(None, ('grp', 'shard')), may hold values 0 or 1
- row_table: float32 [16384, 128], P('shard'), may hold values from -3 to 3
- squared_sums: float32 [16384, 128], P('shard'), may hold values from 0.01 to 1
- w_input: bfloat16 [512, 1024], replicated, may hold values from -0.25 to 0.25
- w_hidden: bfloat16 [1024, 1024], replicated, may hold values from -0.1875 to 0.1875
- w_output: bfloat16 [1024], replicated, may hold values from -0.1875 to 0.1875
Outputs:
- new_table: float32 [16384, 128], P('shard')
- logits: float32 [2, 65536], P(None, ('grp', 'shard'))
- input_grad: float32 [524288], P(('grp', 'shard'))
The draws below stay inside these ranges and needn't reach their ends.
Inputs may be any that keep to these rules, and one draw needn't show every extreme that they name: `owner_shard`: within the ids of one device in one minibatch (aligned blocks of 2048 ids), at most 128 name the same owner shard, and that many do in some block.
All inputs are finite; a program needn't handle non-finite values. No bound on the sum of `click_label` on one device may be relied on, other than what follows from the above.
Results may differ from the reference program's by a relative error of at most 0.0039.
The reference program's roundings to bfloat16 on the way count: a program that leaves them out, or rounds other values in their place, can miss the bound.
Values may be sent and summed in bfloat16 or wider, within the bound.
No kernel may reach another device: no remote copies, remote signals or barrier semaphores. Data moves between devices by JAX's collectives and lax.ppermute only.
A program may use at most 64 MiB of HBM per device.

```python
import math
import jax
import jax.numpy as jnp
import numpy as np
from jax import lax

E = 128
H = 1024
SLOTS = 4
HOT = 4
BATCHES = 2
TOK_DEV = 128
ROW_DEV = 512
LOOK = 16
CAP = 128
TOKENS = 65536
ROWS = 16384
N_SHARD = 32


def set_ends(array, own_key, low, top_value):
    extent = array.shape
    spot = [jax.random.randint(jax.random.fold_in(own_key, axis), (), 0, extent[axis]) for axis in range(len(extent))]
    array = array.at[tuple(spot)].set(low)
    longest = extent.index(max(extent))
    spot[longest] = (spot[longest] + 1) % extent[longest]
    return array.at[tuple(spot)].set(top_value)


def block_scale(stream_key, extent, cuts, smallest, largest):
    loudness = 1.0
    for position, shards_of in cuts:
        heights = jax.random.uniform(jax.random.fold_in(jax.random.fold_in(stream_key, 6), position), (shards_of,), jnp.float32, smallest / len(cuts), largest / len(cuts))
        loudness = loudness * jnp.repeat(jnp.exp(heights), extent[position] // shards_of).reshape((-1,) + (1,) * (len(extent) - 1 - position))
    return loudness


def rank_table(amount, skew):
    portions = [(1 << 20) // math.isqrt(rank ** skew) + 1 for rank in range(1, amount + 1)]
    spread = 1 + sum(portions) // (1 << 30)
    return np.cumsum(np.array([max(1, weight // spread) for weight in portions]))


def ranked_ids(rng, extent, number_of, skew):
    listing = rank_table(number_of, skew)
    ticket = jax.random.randint(jax.random.fold_in(rng, 1), extent, 0, int(listing[number_of - 1]))
    grade = jnp.searchsorted(jnp.asarray(listing, jnp.int32), ticket, side="right")
    return jax.random.permutation(jax.random.fold_in(rng, 2), number_of)[grade].astype(jnp.int32)


def assign_block(own_key, own, number, rows, number_of, top, most, lean):
    sequence = jax.random.permutation(own_key, number_of)
    packed, ordinary = portions_of(number_of, rows * top, most, lean, True), portions_of(number_of, rows * top, most, lean, False)
    places = jnp.arange(number_of)

    def named(sizes, offset_by):
        used = int((sizes > 0).sum())
        fixed = max(1, used // 4)
        shifted = fixed + (places - fixed + offset_by * (used - fixed)) % max(1, number_of - fixed)
        return jnp.zeros((number_of,), jnp.int32).at[sequence[jnp.where(places < fixed, places, shifted)]].set(jnp.asarray(sizes, jnp.int32))

    sizes = jnp.where(number % 4 == 0, named(packed, number // 4), named(ordinary, number - number // 4 - 1))
    mixed = jax.random.permutation(jax.random.fold_in(own, 3), number_of)
    source_of, receiver = mixed[0:number_of // 2 * 2:2], mixed[1:number_of // 2 * 2:2]
    slack = jnp.minimum(sizes[source_of] - 1, most - sizes[receiver]) // 2
    slack = jnp.where((source_of == sequence[0]) | (receiver == sequence[0]) | (sizes[receiver] == 0), 0, jnp.maximum(slack, 0))
    shifted = jax.random.randint(jax.random.fold_in(own, 4), (number_of // 2,), 0, 1 << 20) % (slack + 1)
    sizes = sizes.at[source_of].add(-shifted).at[receiver].add(shifted)
    members = jnp.searchsorted(jnp.cumsum(sizes), jnp.arange(rows * top), side="right").astype(jnp.int32)
    listing = members.reshape(top, rows).T
    listing = listing[jax.random.permutation(jax.random.fold_in(own, 1), rows)]
    offset_by = jax.random.randint(jax.random.fold_in(own, 2), (rows, 1), 0, top)
    return jnp.take_along_axis(listing, (jnp.arange(top)[None, :] + offset_by) % top, axis=1)


def portions_of(count, total, limit, lean, full):
    portions = [(1 << 20) // math.isqrt(rank ** lean) + 1 for rank in range(1, count + 1)]
    largest = limit if full else min(limit, max(-(-total // count), total * portions[0] // sum(portions)))
    least = 1 if total - largest >= count - 1 else 0
    given, rest = [largest] + [least] * (count - 1), total - largest - least * (count - 1)
    while rest > 0:
        movable = [i for i in range(1, count) if given[i] < largest] or [i for i in range(1, count) if given[i] < limit]
        pool, budget = sum([portions[i] for i in movable]), rest
        for i in movable:
            addition = min(limit - given[i], max(1, budget * portions[i] // pool), rest)
            given[i] = given[i] + addition
            rest = rest - addition
    return np.array(given)


def bell_draw(own_key, extent, spread, most, shards=(), held_as=jnp.bfloat16):
    result = jax.random.normal(own_key, extent, jnp.float32) * spread
    if len(shards) > 0:
        result = block_scale(own_key, extent, shards, -0.22, 0.18) * result
    return jnp.clip(result, min=-most, max=most).astype(held_as)


def setup_inputs(seed: int = 0) -> dict:
    key_list = jax.random.split(jax.random.key(seed), 9)
    owner_shard_keys = jax.random.split(jax.random.fold_in(key_list[0], 1), BATCHES * TOKENS * LOOK // (TOK_DEV * LOOK))
    owner_shard_turns = jax.random.permutation(jax.random.fold_in(key_list[0], 3), BATCHES * TOKENS * LOOK // (TOK_DEV * LOOK))
    owner_shard = jax.vmap(lambda own, number: assign_block(jax.random.fold_in(key_list[0], 2), own, number, TOK_DEV * LOOK, N_SHARD, 1, CAP, 2))(owner_shard_keys, owner_shard_turns).reshape((BATCHES, TOKENS, LOOK, 1))
    local_row = set_ends(ranked_ids(key_list[1], (BATCHES, TOKENS, LOOK), ROW_DEV, 2), jax.random.fold_in(key_list[1], 3), 0, ROW_DEV - 1).astype(jnp.int32)
    click_label = set_ends((jax.random.randint(key_list[2], (BATCHES, TOKENS), 0, 4) < 1).astype(jnp.int32), jax.random.fold_in(key_list[2], 1), 0, 1)
    row_table = bell_draw(key_list[3], (ROWS, E), 0.5, 3.0, ((0, 32),), jnp.float32)
    squared_sums = jnp.clip(jnp.exp(math.log(1.0) - 4.6051702 * jax.random.uniform(key_list[4], (ROWS, E), jnp.float32) ** block_scale(key_list[4], (ROWS, E), ((0, 32),), -0.2, 0.2)), 0.01, 1.0)
    w_input = bell_draw(key_list[5], (SLOTS * E, H), (SLOTS * E) ** -0.5, 0.25)
    w_hidden = bell_draw(key_list[6], (H, H), H ** -0.5, 0.1875)
    w_output = bell_draw(key_list[7], (H,), H ** -0.5, 0.1875)
    return dict(owner_shard=owner_shard, local_row=local_row, click_label=click_label, row_table=row_table, squared_sums=squared_sums, w_input=w_input, w_hidden=w_hidden, w_output=w_output)


learn_rate = 0.1

def mlp_pass(rows, labels, w_input, w_hidden, w_output):
    count = rows.shape[0]
    width = rows.shape[2]
    pooled = lax.optimization_barrier(jnp.sum(rows.reshape(count, SLOTS, HOT, width), axis=2, dtype=jnp.float32))
    pooled = pooled.astype(jnp.bfloat16).reshape(count, SLOTS * width)
    pre_one = jnp.dot(pooled, w_input, preferred_element_type=jnp.float32)
    act_one = jnp.maximum(pre_one, 0.0).astype(jnp.bfloat16)
    pre_two = jnp.dot(act_one, w_hidden, preferred_element_type=jnp.float32)
    act_two = jnp.maximum(pre_two, 0.0).astype(jnp.bfloat16)
    logits = jnp.dot(act_two, w_output, preferred_element_type=jnp.float32)
    slope = jax.nn.sigmoid(logits) - labels
    back_two = jnp.where(pre_two > 0, slope[:, None] * w_output.astype(jnp.float32)[None, :], 0.0).astype(jnp.bfloat16)
    back_one = lax.dot_general(back_two, w_hidden, (((1,), (1,)), ((), ())), preferred_element_type=jnp.float32)
    back_one = jnp.where(pre_one > 0, back_one, 0.0).astype(jnp.bfloat16)
    back_in = lax.dot_general(back_one, w_input, (((1,), (1,)), ((), ())), preferred_element_type=jnp.float32)
    back_in = back_in.astype(jnp.bfloat16)
    weight_term = lax.dot_general(pooled, back_one, (((0,), (0,)), ((), ())), preferred_element_type=jnp.float32)
    lookup_grad = jnp.broadcast_to(back_in.reshape(count, SLOTS, 1, width), (count, SLOTS, HOT, width))
    return (logits, lookup_grad.reshape(count * SLOTS * HOT, width), weight_term)

def reference(owner_shard, local_row, click_label, row_table, squared_sums, w_input, w_hidden, w_output):
    table_low = row_table.astype(jnp.bfloat16)
    global_id = (owner_shard[..., 0] * ROW_DEV + local_row).astype(jnp.int32)
    block = TOK_DEV * N_SHARD
    count = BATCHES * TOKENS // block
    id_blocks = global_id.reshape(count, block, LOOK)
    label_blocks = click_label.astype(jnp.float32).reshape(count, block)

    def one_block(carry, inputs):
        ids, labels = inputs
        grads, weights = carry
        logits, lookup_grad, weight_term = mlp_pass(table_low[ids], labels, w_input, w_hidden, w_output)
        grads = grads + jax.ops.segment_sum(lookup_grad.astype(jnp.float32), ids.reshape(-1), num_segments=ROWS)
        return ((grads, weights + weight_term), logits)
    start = (jnp.zeros((ROWS, E), jnp.float32), jnp.zeros((SLOTS * E, H), jnp.float32))
    (row_grad, input_grad), logits = lax.scan(one_block, start, (id_blocks, label_blocks))
    new_sums = squared_sums + row_grad * row_grad
    new_table = row_table - learn_rate * row_grad / jnp.sqrt(new_sums)
    return (new_table, logits.reshape(BATCHES, TOKENS), input_grad.reshape(-1))
```

```python
import jax
import jax.numpy as jnp
from jax import lax
from jax.experimental import pallas as pl
from jax.experimental.pallas import tpu as pltpu
from jax.sharding import PartitionSpec as P

bf16 = jnp.bfloat16
f32 = jnp.float32
learn_rate = 0.1

SLOTS = 4
HOT = 4
LOOK = 16
SHARDS = 32
CAP = 128
BATCHES = 2
GRAD_ROWS = BATCHES * CAP
TERM_ROWS = 128
ID_ROWS = 16
SENT_ROWS = GRAD_ROWS + TERM_ROWS + ID_ROWS

FIRST = [[x * 8 + y * 2 for x in range(4)] for y in range(4)] + [
    [x * 8 + y * 2 + 1 for y in range(4)] for x in range(4)
]
SECOND = [[x * 8 + y * 2 for y in range(4)] for x in range(4)] + [
    [x * 8 + y * 2 + 1 for x in range(4)] for y in range(4)
]
SWAP = [(i, i ^ 1) for i in range(SHARDS)]
NEAR = [[4 * i + j for j in range(4)] for i in range(4)]
FAR = [[4 * i + j for i in range(4)] for j in range(4)]


def exchange(value, axis, groups=None):
    return lax.all_to_all(
        value, axis, split_axis=0, concat_axis=0, tiled=True, axis_index_groups=groups
    )


def spread(value, axis, groups):
    return exchange(jnp.broadcast_to(value[None], (4,) + value.shape), axis, groups)


def gather_table(table_low):
    rows, width = table_low.shape
    line = spread(table_low, "shard", FIRST).reshape(4 * rows, width)
    own = spread(line, "shard", SECOND).reshape(16 * rows, width)
    other = lax.ppermute(own, "shard", SWAP)
    return own, other


def dot(a, b, dims):
    return lax.dot_general(a, b, (dims, ((), ())), preferred_element_type=f32)


def column(row):
    return jnp.transpose(jnp.broadcast_to(row, (128, 128)))[:, 0:1]


def main_kernel(
    index_ref,
    place_ref,
    own_ref,
    other_ref,
    label_ref,
    w_input_ref,
    w_hidden_ref,
    w_output_ref,
    ids_ref,
    sent_ref,
    logit_ref,
    table_ref,
    pooled_ref,
    slot_ref,
    term_ref,
):
    half = own_ref.shape[0]
    samples = pooled_ref.shape[0] // SLOTS

    def widen(step, carry):
        at = pl.multiple_of(step * 256, 256)
        table_ref[pl.ds(at, 256), :] = own_ref[pl.ds(at, 256), :].astype(f32)
        table_ref[pl.ds(half + at, 256), :] = other_ref[pl.ds(at, 256), :].astype(f32)
        return carry

    lax.fori_loop(0, half // 256, widen, 0)

    def look(sample, carry):
        for slot in range(SLOTS):
            first = sample * LOOK + slot * HOT
            total = table_ref[pl.ds(index_ref[first], 1), :]
            for hot in range(1, HOT):
                total = total + table_ref[pl.ds(index_ref[first + hot], 1), :]
            pooled_ref[pl.ds(slot * samples + sample, 1), :] = total
        return carry

    lax.fori_loop(0, samples, look, 0, unroll=4)

    def clear(step, carry):
        slot_ref[pl.ds(pl.multiple_of(step * 256, 256), 256), :] = jnp.zeros((256, 128), f32)
        return carry

    lax.fori_loop(0, slot_ref.shape[0] // 256, clear, 0)

    pooled = jnp.concatenate(
        [pooled_ref[slot * samples : (slot + 1) * samples, :].astype(bf16) for slot in range(SLOTS)],
        axis=1,
    )
    w_input = w_input_ref[...]
    w_hidden = w_hidden_ref[...]
    w_output = w_output_ref[...].astype(f32)
    labels = jnp.concatenate([column(label_ref[b : b + 1, :]) for b in range(BATCHES)], axis=0)
    pre_one = dot(pooled, w_input, ((1,), (0,)))
    act_one = jnp.maximum(pre_one, 0.0).astype(bf16)
    pre_two = dot(act_one, w_hidden, ((1,), (0,)))
    act_two = jnp.maximum(pre_two, 0.0).astype(bf16).astype(f32)
    logits = jnp.sum(act_two * w_output, axis=1, keepdims=True)
    for b in range(BATCHES):
        part = jnp.broadcast_to(logits[b * 128 : (b + 1) * 128], (128, 128))
        logit_ref[b : b + 1, :] = jnp.transpose(part)[0:1, :]
    slope = jax.nn.sigmoid(logits) - labels
    back_two = jnp.where(pre_two > 0, slope * w_output, 0.0).astype(bf16)
    back_one = dot(back_two, w_hidden, ((1,), (1,)))
    back_one = jnp.where(pre_one > 0, back_one, 0.0).astype(bf16)
    back_in = dot(back_one, w_input, ((1,), (1,))).astype(bf16).astype(f32)
    for slot in range(SLOTS):
        pooled_ref[slot * samples : (slot + 1) * samples, :] = back_in[:, slot * 128 : (slot + 1) * 128]
    inner = pooled.shape[1]
    for j in range(term_ref.shape[0] // inner):
        term_ref[j * inner : (j + 1) * inner, :] = dot(
            pooled, back_one[:, j * 128 : (j + 1) * 128], ((0,), (0,))
        )

    def scatter(sample, carry):
        for slot in range(SLOTS):
            first = sample * LOOK + slot * HOT
            row = pooled_ref[pl.ds(slot * samples + sample, 1), :]
            for hot in range(HOT):
                slot_ref[pl.ds(place_ref[first + hot], 1), :] = row
        return carry

    lax.fori_loop(0, samples, scatter, 0, unroll=4)

    def pack(owner, carry):
        at = pl.multiple_of(owner * GRAD_ROWS, GRAD_ROWS)
        sent_ref[owner, 0:GRAD_ROWS, :] = slot_ref[pl.ds(at, GRAD_ROWS), :].astype(bf16)
        sent_ref[owner, GRAD_ROWS : GRAD_ROWS + TERM_ROWS, :] = term_ref[
            pl.ds(owner, TERM_ROWS, stride=SHARDS), :
        ].astype(bf16)
        sent_ref[owner, GRAD_ROWS + TERM_ROWS : SENT_ROWS, :] = ids_ref[owner]
        return carry

    lax.fori_loop(0, SHARDS, pack, 0)


def run_main(index, place, own, other, labels, w_input, w_hidden, w_output, ids):
    width = own.shape[1]
    samples = index.shape[0] // LOOK
    smem = pl.BlockSpec(memory_space=pltpu.SMEM)
    vmem = pl.BlockSpec(memory_space=pltpu.VMEM)
    return pl.pallas_call(
        main_kernel,
        out_shape=(
            jax.ShapeDtypeStruct((SHARDS, SENT_ROWS, width), bf16),
            jax.ShapeDtypeStruct((BATCHES, samples // BATCHES), f32),
        ),
        in_specs=[smem, smem] + [vmem] * 7,
        out_specs=(vmem, vmem),
        scratch_shapes=[
            pltpu.VMEM((2 * own.shape[0], width), f32),
            pltpu.VMEM((samples * SLOTS, width), f32),
            pltpu.VMEM((SHARDS * GRAD_ROWS, width), f32),
            pltpu.VMEM((SHARDS * TERM_ROWS, width), f32),
        ],
        compiler_params=pltpu.CompilerParams(vmem_limit_bytes=50 * 1024 * 1024),
        cost_estimate=pl.CostEstimate(
            flops=2_000_000_000, bytes_accessed=12_000_000, transcendentals=256
        ),
    )(index, place, own, other, labels, w_input, w_hidden, w_output, ids)


def owner_kernel(got_ref, out_ref, sum_ref, term_ref):
    step = pl.program_id(0)

    @pl.when(step == 0)
    def _():
        sum_ref[...] = jnp.zeros_like(sum_ref)
        term_ref[...] = jnp.zeros_like(term_ref)

    names = lax.broadcasted_iota(jnp.int32, (sum_ref.shape[0], CAP), 0).astype(f32) + 1.0
    total = sum_ref[...]
    term = term_ref[...]
    for source in range(got_ref.shape[0]):
        coded = got_ref[source, GRAD_ROWS + TERM_ROWS : SENT_ROWS, :].astype(f32)
        picks = []
        for b in range(BATCHES):
            named = coded[b : b + 1] * 256.0 + coded[BATCHES + b : BATCHES + b + 1]
            picks.append(jnp.where(names == named, 1.0, 0.0).astype(bf16))
        pick = jnp.concatenate(picks, axis=1)
        total = total + dot(pick, got_ref[source, 0:GRAD_ROWS, :], ((1,), (0,)))
        term = term + got_ref[source, GRAD_ROWS : GRAD_ROWS + TERM_ROWS, :].astype(f32)
    sum_ref[...] = total
    term_ref[...] = term

    @pl.when(step == pl.num_programs(0) - 1)
    def _():
        for k in range(4):
            out_ref[k, 0:128, :] = sum_ref[k * 128 : (k + 1) * 128, :].astype(bf16)
            part = term_ref[pl.ds(k, 32, stride=4), :]
            high = part.astype(bf16)
            out_ref[k, 128:160, :] = high
            out_ref[k, 160:192, :] = (part - high.astype(f32)).astype(bf16)


def run_owner(got, rows):
    width = got.shape[2]
    return pl.pallas_call(
        owner_kernel,
        grid=(8,),
        out_shape=jax.ShapeDtypeStruct((4, 192, width), bf16),
        in_specs=[pl.BlockSpec((SHARDS // 8, SENT_ROWS, width), lambda i: (i, 0, 0))],
        out_specs=pl.BlockSpec((4, 192, width), lambda i: (0, 0, 0)),
        scratch_shapes=[
            pltpu.VMEM((rows, width), f32),
            pltpu.VMEM((TERM_ROWS, width), f32),
        ],
        compiler_params=pltpu.CompilerParams(vmem_limit_bytes=32 * 1024 * 1024),
        cost_estimate=pl.CostEstimate(
            flops=1_100_000_000, bytes_accessed=3_500_000, transcendentals=0
        ),
    )(got)


def plan_slots(owner, row):
    batches, samples, looks = owner.shape
    names = jnp.arange(SHARDS, dtype=jnp.int32)
    hit = (owner[..., None] == names).astype(bf16).reshape(batches, samples, looks * SHARDS)
    steps = jnp.arange(samples)
    before = (steps[None, :] < steps[:, None]).astype(bf16)
    rank = jnp.einsum("ts,bsn->btn", before, hit, preferred_element_type=f32)
    counts = jnp.sum(hit.astype(f32), axis=1).reshape(batches, looks, SHARDS)
    turn = jnp.arange(looks)
    base = jnp.sum(
        jnp.where((turn[None, :] < turn[:, None])[None, :, :, None], counts[:, None], 0.0), axis=2
    ).reshape(batches, 1, looks * SHARDS)
    spot = jnp.sum(
        (hit.astype(f32) * (rank + base)).reshape(batches, samples, looks, SHARDS), axis=3
    ).astype(jnp.int32)
    batch = jnp.arange(batches, dtype=jnp.int32)[:, None, None]
    place = owner * GRAD_ROWS + batch * CAP + spot
    code = row + 1
    high = (code >> 8).astype(bf16)
    low = (code & 255).astype(bf16)
    flat_hit = hit.reshape(batches, samples * looks, SHARDS)
    coded = jnp.concatenate(
        [flat_hit * high.reshape(batches, -1, 1), flat_hit * low.reshape(batches, -1, 1)], axis=2
    )
    where = (spot.reshape(batches, -1, 1) == jnp.arange(CAP, dtype=jnp.int32)).astype(bf16)
    ids = jnp.einsum("bin,bip->bnp", coded, where, preferred_element_type=f32).astype(bf16)
    ids = ids.reshape(batches, 2, SHARDS, CAP).transpose(2, 1, 0, 3).reshape(SHARDS, 2 * batches, CAP)
    ids = jnp.pad(ids, ((0, 0), (0, ID_ROWS - 2 * batches), (0, 0)))
    return place.reshape(-1), ids


def table_index(owner, row, rows):
    core = lax.axis_index("shard") & 1
    x, y, c = owner >> 3, (owner >> 1) & 3, owner & 1
    chip = jnp.where(c == 0, y * 4 + x, x * 4 + y)
    return (((c ^ core) * 16 + chip) * rows + row).reshape(-1)


def adagrad_step(table_part, sums_part, grad_part):
    new_sums = sums_part + grad_part * grad_part
    return table_part - learn_rate * grad_part / jnp.sqrt(new_sums)


def local(
    owner_shard, local_row, click_label, row_table, squared_sums, w_input, w_hidden, w_output
):
    rows, width = row_table.shape
    owner = owner_shard[..., 0]
    own, other = gather_table(row_table.astype(bf16))
    index = table_index(owner, local_row, rows)
    place, ids = plan_slots(owner, local_row)
    sent, logits = run_main(
        index,
        place,
        own,
        other,
        click_label.astype(f32),
        w_input,
        w_hidden,
        w_output.reshape(1, -1),
        ids,
    )
    near = exchange(run_owner(exchange(sent, "shard"), rows), "grp", NEAR).astype(f32)
    grads = jnp.sum(near[:, 0:128], axis=0).astype(bf16)
    term = jnp.sum(near[:, 128:160] + near[:, 160:192], axis=0)
    term = term.reshape(8, 4, width).transpose(1, 0, 2)
    high = term.astype(bf16)
    low = (term - high.astype(f32)).astype(bf16)
    far = jnp.concatenate([jnp.broadcast_to(grads[None], (4, 128, width)), high, low], axis=1)
    far = exchange(far, "grp", FAR).astype(f32)
    input_grad = jnp.sum(far[:, 128:136] + far[:, 136:144], axis=0).reshape(-1)
    part = jnp.sum(far[:, 0:128], axis=0).astype(bf16)
    total = spread(part, "grp", NEAR).reshape(rows, width).astype(f32)
    new_table = adagrad_step(row_table, squared_sums, total)
    return (new_table, logits, input_grad)


def solution(mesh):
    in_specs = (
        P(None, ("grp", "shard"), None, None),
        P(None, ("grp", "shard"), None),
        P(None, ("grp", "shard")),
        P("shard", None),
        P("shard", None),
        P(),
        P(),
        P(),
    )
    out_specs = (P("shard", None), P(None, ("grp", "shard")), P(("grp", "shard")))
    return jax.shard_map(local, mesh=mesh, in_specs=in_specs, out_specs=out_specs, check_vma=False)
```

```python
import jax
import jax.numpy as jnp
from jax import lax
from jax.experimental import pallas as pl
from jax.experimental.pallas import tpu as pltpu
from jax.sharding import PartitionSpec as P

bf16 = jnp.bfloat16
f32 = jnp.float32
learn_rate = 0.1

SLOTS = 4
HOT = 4
LOOK = 16
SHARDS = 32
CAP = 128
BATCHES = 2
GRAD_ROWS = BATCHES * CAP
TERM_ROWS = 128
ID_ROWS = 16
SENT_ROWS = GRAD_ROWS + TERM_ROWS + ID_ROWS

FIRST = [[x * 8 + y * 2 for x in range(4)] for y in range(4)] + [
    [x * 8 + y * 2 + 1 for y in range(4)] for x in range(4)
]
SECOND = [[x * 8 + y * 2 for y in range(4)] for x in range(4)] + [
    [x * 8 + y * 2 + 1 for x in range(4)] for y in range(4)
]
SWAP = [(i, i ^ 1) for i in range(SHARDS)]
NEAR = [[4 * i + j for j in range(4)] for i in range(4)]
FAR = [[4 * i + j for i in range(4)] for j in range(4)]


def exchange(value, axis, groups=None):
    return lax.all_to_all(
        value, axis, split_axis=0, concat_axis=0, tiled=True, axis_index_groups=groups
    )


def spread(value, axis, groups):
    return exchange(jnp.broadcast_to(value[None], (4,) + value.shape), axis, groups)


def gather_table(table_low):
    rows, width = table_low.shape
    line = spread(table_low, "shard", FIRST).reshape(4 * rows, width)
    own = spread(line, "shard", SECOND).reshape(16 * rows, width)
    other = lax.ppermute(own, "shard", SWAP)
    return own, other


def dot(a, b, dims):
    return lax.dot_general(a, b, (dims, ((), ())), preferred_element_type=f32)


def column(row):
    return jnp.transpose(jnp.broadcast_to(row, (128, 128)))[:, 0:1]


def main_kernel(
    index_ref,
    place_ref,
    own_hbm,
    other_hbm,
    label_ref,
    w_input_hbm,
    w_hidden_hbm,
    w_output_ref,
    ids_ref,
    sent_hbm,
    logit_ref,
    half_ref,
    w_input_ref,
    w_hidden_ref,
    table_ref,
    pooled_ref,
    slot_ref,
    turn_ref,
    term_ref,
    sent_ref,
    half_sem,
    weight_sem,
    sent_sem,
):
    half = own_hbm.shape[0]
    chunk = half // 2
    samples = pooled_ref.shape[0] // SLOTS
    tables = []
    for k in range(4):
        source = (own_hbm, other_hbm)[k // 2].at[pl.ds((k % 2) * chunk, chunk)]
        tables.append(
            pltpu.make_async_copy(source, half_ref.at[pl.ds(k * chunk, chunk)], half_sem.at[k])
        )
    weights = [
        pltpu.make_async_copy(w_input_hbm, w_input_ref, weight_sem.at[0]),
        pltpu.make_async_copy(w_hidden_hbm, w_hidden_ref, weight_sem.at[1]),
    ]
    for copy in tables + weights:
        copy.start()

    def clear(step, carry):
        slot_ref[pl.ds(pl.multiple_of(step * 256, 256), 256), :] = jnp.zeros((256, 128), f32)
        return carry

    lax.fori_loop(0, slot_ref.shape[0] // 256, clear, 0)

    def widen(step, carry):
        at = pl.multiple_of(step * 256, 256)
        table_ref[pl.ds(at, 256), :] = half_ref[pl.ds(at, 256), :].astype(f32)
        return carry

    for k in range(4):
        tables[k].wait()
        lax.fori_loop(k * chunk // 256, (k + 1) * chunk // 256, widen, 0)

    def look(sample, carry):
        for slot in range(SLOTS):
            first = sample * LOOK + slot * HOT
            total = table_ref[pl.ds(index_ref[first], 1), :]
            for hot in range(1, HOT):
                total = total + table_ref[pl.ds(index_ref[first + hot], 1), :]
            pooled_ref[pl.ds(slot * samples + sample, 1), :] = total
        return carry

    lax.fori_loop(0, samples, look, 0, unroll=16)

    features = SLOTS * 128
    for slot in range(SLOTS):
        for b in range(BATCHES):
            block = pooled_ref[slot * samples + b * 128 : slot * samples + (b + 1) * 128, :]
            turn_ref[b * features + slot * 128 : b * features + (slot + 1) * 128, :] = jnp.transpose(block)
    turned = jnp.concatenate(
        [
            jnp.concatenate(
                [turn_ref[pl.ds(b * features + s, 16, stride=SHARDS), :] for s in range(SHARDS)],
                axis=0,
            ).astype(bf16)
            for b in range(BATCHES)
        ],
        axis=1,
    )
    pooled = jnp.concatenate(
        [pooled_ref[slot * samples : (slot + 1) * samples, :].astype(bf16) for slot in range(SLOTS)],
        axis=1,
    )
    for copy in weights:
        copy.wait()
    w_input = w_input_ref[...]
    w_hidden = w_hidden_ref[...]
    w_output = w_output_ref[...].astype(f32)
    labels = jnp.concatenate([column(label_ref[b : b + 1, :]) for b in range(BATCHES)], axis=0)
    pre_one = dot(pooled, w_input, ((1,), (0,)))
    act_one = jnp.maximum(pre_one, 0.0).astype(bf16)
    pre_two = dot(act_one, w_hidden, ((1,), (0,)))
    act_two = jnp.maximum(pre_two, 0.0).astype(bf16).astype(f32)
    logits = jnp.sum(act_two * w_output, axis=1, keepdims=True)
    for b in range(BATCHES):
        part = jnp.broadcast_to(logits[b * 128 : (b + 1) * 128], (128, 128))
        logit_ref[b : b + 1, :] = jnp.transpose(part)[0:1, :]
    slope = jax.nn.sigmoid(logits) - labels
    back_two = jnp.where(pre_two > 0, slope * w_output, 0.0).astype(bf16)
    back_one = dot(back_two, w_hidden, ((1,), (1,)))
    back_one = jnp.where(pre_one > 0, back_one, 0.0).astype(bf16)
    back_in = dot(back_one, w_input, ((1,), (1,))).astype(bf16).astype(f32)
    for slot in range(SLOTS):
        pooled_ref[slot * samples : (slot + 1) * samples, :] = back_in[:, slot * 128 : (slot + 1) * 128]
    term_ref[...] = dot(turned, back_one, ((1,), (0,)))

    def scatter(sample, carry):
        for slot in range(SLOTS):
            first = sample * LOOK + slot * HOT
            row = pooled_ref[pl.ds(slot * samples + sample, 1), :]
            for hot in range(HOT):
                slot_ref[pl.ds(place_ref[first + hot], 1), :] = row
        return carry

    lax.fori_loop(0, samples, scatter, 0, unroll=16)

    def pack(owner, carry):
        at = pl.multiple_of(owner * GRAD_ROWS, GRAD_ROWS)
        sent_ref[owner, 0:GRAD_ROWS, :] = slot_ref[pl.ds(at, GRAD_ROWS), :].astype(bf16)
        piece = term_ref[pl.ds(pl.multiple_of(owner * 16, 16), 16), :].astype(bf16)
        for j in range(8):
            sent_ref[owner, GRAD_ROWS + j * 16 : GRAD_ROWS + (j + 1) * 16, :] = piece[
                :, j * 128 : (j + 1) * 128
            ]
        sent_ref[owner, GRAD_ROWS + TERM_ROWS : SENT_ROWS, :] = ids_ref[owner]
        return carry

    parts = 4
    step = SHARDS // parts
    stores = []
    for k in range(parts):
        lax.fori_loop(k * step, (k + 1) * step, pack, 0, unroll=4)
        piece = pl.ds(k * step, step)
        stores.append(
            pltpu.make_async_copy(sent_ref.at[piece], sent_hbm.at[piece], sent_sem.at[k])
        )
        stores[-1].start()
    for copy in stores:
        copy.wait()


def run_main(index, place, own, other, labels, w_input, w_hidden, w_output, ids):
    width = own.shape[1]
    samples = index.shape[0] // LOOK
    smem = pl.BlockSpec(memory_space=pltpu.SMEM)
    vmem = pl.BlockSpec(memory_space=pltpu.VMEM)
    anywhere = pl.BlockSpec(memory_space=pl.ANY)
    return pl.pallas_call(
        main_kernel,
        out_shape=(
            jax.ShapeDtypeStruct((SHARDS, SENT_ROWS, width), bf16),
            jax.ShapeDtypeStruct((BATCHES, samples // BATCHES), f32),
        ),
        in_specs=[smem, smem, anywhere, anywhere, vmem, anywhere, anywhere, vmem, vmem],
        out_specs=(anywhere, vmem),
        scratch_shapes=[
            pltpu.VMEM((2 * own.shape[0], width), bf16),
            pltpu.VMEM(w_input.shape, bf16),
            pltpu.VMEM(w_hidden.shape, bf16),
            pltpu.VMEM((2 * own.shape[0], width), f32),
            pltpu.VMEM((samples * SLOTS, width), f32),
            pltpu.VMEM((SHARDS * GRAD_ROWS, width), f32),
            pltpu.VMEM((BATCHES * SLOTS * width, samples // BATCHES), f32),
            pltpu.VMEM(w_input.shape, f32),
            pltpu.VMEM((SHARDS, SENT_ROWS, width), bf16),
            pltpu.SemaphoreType.DMA((4,)),
            pltpu.SemaphoreType.DMA((2,)),
            pltpu.SemaphoreType.DMA((4,)),
        ],
        compiler_params=pltpu.CompilerParams(vmem_limit_bytes=40 * 1024 * 1024),
        cost_estimate=pl.CostEstimate(
            flops=2_000_000_000, bytes_accessed=12_000_000, transcendentals=256
        ),
    )(index, place, own, other, labels, w_input, w_hidden, w_output, ids)


def owner_kernel(got_ref, out_ref, sum_ref, term_ref):
    step = pl.program_id(0)

    @pl.when(step == 0)
    def _():
        sum_ref[...] = jnp.zeros_like(sum_ref)
        term_ref[...] = jnp.zeros_like(term_ref)

    names = lax.broadcasted_iota(jnp.int32, (sum_ref.shape[0], CAP), 0).astype(f32) + 1.0
    total = sum_ref[...]
    term = term_ref[...]
    for source in range(got_ref.shape[0]):
        coded = got_ref[source, GRAD_ROWS + TERM_ROWS : SENT_ROWS, :].astype(f32)
        picks = []
        for b in range(BATCHES):
            named = coded[b : b + 1] * 256.0 + coded[BATCHES + b : BATCHES + b + 1]
            picks.append(jnp.where(names == named, 1.0, 0.0).astype(bf16))
        pick = jnp.concatenate(picks, axis=1)
        total = total + dot(pick, got_ref[source, 0:GRAD_ROWS, :], ((1,), (0,)))
        term = term + got_ref[source, GRAD_ROWS : GRAD_ROWS + TERM_ROWS, :].astype(f32)
    sum_ref[...] = total
    term_ref[...] = term

    @pl.when(step == pl.num_programs(0) - 1)
    def _():
        for k in range(4):
            out_ref[k, 0:128, :] = sum_ref[k * 128 : (k + 1) * 128, :].astype(bf16)
            part = term_ref[pl.ds(k, 32, stride=4), :]
            out_ref[k, 128:160, :] = part.astype(bf16)


def run_owner(got, rows):
    width = got.shape[2]
    return pl.pallas_call(
        owner_kernel,
        grid=(8,),
        out_shape=jax.ShapeDtypeStruct((4, 160, width), bf16),
        in_specs=[pl.BlockSpec((SHARDS // 8, SENT_ROWS, width), lambda i: (i, 0, 0))],
        out_specs=pl.BlockSpec((4, 160, width), lambda i: (0, 0, 0)),
        scratch_shapes=[
            pltpu.VMEM((rows, width), f32),
            pltpu.VMEM((TERM_ROWS, width), f32),
        ],
        compiler_params=pltpu.CompilerParams(vmem_limit_bytes=32 * 1024 * 1024),
        cost_estimate=pl.CostEstimate(
            flops=1_100_000_000, bytes_accessed=3_500_000, transcendentals=0
        ),
    )(got)


def plan_slots(owner, row):
    batches, samples, looks = owner.shape
    names = jnp.arange(SHARDS, dtype=jnp.int32)
    hit = (owner[..., None] == names).astype(bf16).reshape(batches, samples, looks * SHARDS)
    steps = jnp.arange(samples)
    before = (steps[None, :] < steps[:, None]).astype(bf16)
    rank = jnp.einsum("ts,bsn->btn", before, hit, preferred_element_type=f32)
    counts = jnp.sum(hit.astype(f32), axis=1).reshape(batches, looks, SHARDS)
    turn = jnp.arange(looks)
    base = jnp.sum(
        jnp.where((turn[None, :] < turn[:, None])[None, :, :, None], counts[:, None], 0.0), axis=2
    ).reshape(batches, 1, looks * SHARDS)
    spot = jnp.sum(
        (hit.astype(f32) * (rank + base)).reshape(batches, samples, looks, SHARDS), axis=3
    ).astype(jnp.int32)
    batch = jnp.arange(batches, dtype=jnp.int32)[:, None, None]
    place = owner * GRAD_ROWS + batch * CAP + spot
    code = row + 1
    high = (code >> 8).astype(bf16)
    low = (code & 255).astype(bf16)
    flat_hit = hit.reshape(batches, samples * looks, SHARDS)
    coded = jnp.concatenate(
        [flat_hit * high.reshape(batches, -1, 1), flat_hit * low.reshape(batches, -1, 1)], axis=2
    )
    where = (spot.reshape(batches, -1, 1) == jnp.arange(CAP, dtype=jnp.int32)).astype(bf16)
    ids = jnp.einsum("bin,bip->bnp", coded, where, preferred_element_type=f32).astype(bf16)
    ids = ids.reshape(batches, 2, SHARDS, CAP).transpose(2, 1, 0, 3).reshape(SHARDS, 2 * batches, CAP)
    ids = jnp.pad(ids, ((0, 0), (0, ID_ROWS - 2 * batches), (0, 0)))
    return place.reshape(-1), ids


def table_index(owner, row, rows):
    core = lax.axis_index("shard") & 1
    x, y, c = owner >> 3, (owner >> 1) & 3, owner & 1
    chip = jnp.where(c == 0, y * 4 + x, x * 4 + y)
    return (((c ^ core) * 16 + chip) * rows + row).reshape(-1)


def adagrad_step(table_part, sums_part, grad_part):
    new_sums = sums_part + grad_part * grad_part
    return table_part - learn_rate * grad_part / jnp.sqrt(new_sums)


def local(
    owner_shard, local_row, click_label, row_table, squared_sums, w_input, w_hidden, w_output
):
    rows, width = row_table.shape
    owner = owner_shard[..., 0]
    own, other = gather_table(row_table.astype(bf16))
    index = table_index(owner, local_row, rows)
    place, ids = plan_slots(owner, local_row)
    sent, logits = run_main(
        index,
        place,
        own,
        other,
        click_label.astype(f32),
        w_input,
        w_hidden,
        w_output.reshape(1, -1),
        ids,
    )
    near = exchange(run_owner(exchange(sent, "shard"), rows), "grp", NEAR).astype(f32)
    grads = jnp.sum(near[:, 0:128], axis=0).astype(bf16)
    term = jnp.sum(near[:, 128:160], axis=0)
    term = term.reshape(8, 4, width).transpose(1, 0, 2).astype(bf16)
    far = jnp.concatenate([jnp.broadcast_to(grads[None], (4, 128, width)), term], axis=1)
    far = exchange(far, "grp", FAR).astype(f32)
    input_grad = jnp.sum(far[:, 128:136], axis=0).reshape(-1)
    part = jnp.sum(far[:, 0:128], axis=0).astype(bf16)
    total = spread(part, "grp", NEAR).reshape(rows, width).astype(f32)
    new_table = adagrad_step(row_table, squared_sums, total)
    return (new_table, logits, input_grad)


def solution(mesh):
    in_specs = (
        P(None, ("grp", "shard"), None, None),
        P(None, ("grp", "shard"), None),
        P(None, ("grp", "shard")),
        P("shard", None),
        P("shard", None),
        P(),
        P(),
        P(),
    )
    out_specs = (P("shard", None), P(None, ("grp", "shard")), P(("grp", "shard")))
    return jax.shard_map(local, mesh=mesh, in_specs=in_specs, out_specs=out_specs, check_vma=False)
```

```python
import jax
import jax.numpy as jnp
from jax import lax
from jax.experimental import pallas as pl
from jax.experimental.pallas import tpu as pltpu
from jax.sharding import PartitionSpec as P

bf16 = jnp.bfloat16
f32 = jnp.float32
learn_rate = 0.1

SLOTS = 4
HOT = 4
LOOK = 16
SHARDS = 32
CAP = 128
BATCHES = 2
GRAD_ROWS = BATCHES * CAP
TERM_ROWS = 128
ID_ROWS = 16
SENT_ROWS = GRAD_ROWS + TERM_ROWS + ID_ROWS

FIRST = [[x * 8 + y * 2 for x in range(4)] for y in range(4)] + [
    [x * 8 + y * 2 + 1 for y in range(4)] for x in range(4)
]
SECOND = [[x * 8 + y * 2 for y in range(4)] for x in range(4)] + [
    [x * 8 + y * 2 + 1 for x in range(4)] for y in range(4)
]
SWAP = [(i, i ^ 1) for i in range(SHARDS)]
NEAR = [[4 * i + j for j in range(4)] for i in range(4)]
FAR = [[4 * i + j for i in range(4)] for j in range(4)]


def exchange(value, axis, groups=None):
    return lax.all_to_all(
        value, axis, split_axis=0, concat_axis=0, tiled=True, axis_index_groups=groups
    )


def spread(value, axis, groups):
    return exchange(jnp.broadcast_to(value[None], (4,) + value.shape), axis, groups)


def gather_table(table_low):
    rows, width = table_low.shape
    line = spread(table_low, "shard", FIRST).reshape(4 * rows, width)
    own = spread(line, "shard", SECOND).reshape(16 * rows, width)
    other = lax.ppermute(own, "shard", SWAP)
    return own, other


def dot(a, b, dims):
    return lax.dot_general(a, b, (dims, ((), ())), preferred_element_type=f32)


def column(row):
    return jnp.transpose(jnp.broadcast_to(row, (128, 128)))[:, 0:1]


def main_kernel(
    index_ref,
    place_ref,
    order_ref,
    own_hbm,
    other_hbm,
    label_ref,
    w_input_hbm,
    w_hidden_hbm,
    w_output_ref,
    ids_ref,
    kept_hbm,
    sent_hbm,
    logit_ref,
    half_ref,
    w_input_ref,
    w_hidden_ref,
    table_ref,
    pooled_ref,
    slot_ref,
    turn_ref,
    term_ref,
    sent_ref,
    half_sem,
    weight_sem,
    sent_sem,
):
    half = own_hbm.shape[0]
    chunk = half // 2
    samples = pooled_ref.shape[0] // SLOTS
    tables = []
    for k in range(4):
        source = (own_hbm, other_hbm)[k // 2].at[pl.ds((k % 2) * chunk, chunk)]
        tables.append(
            pltpu.make_async_copy(source, half_ref.at[pl.ds(k * chunk, chunk)], half_sem.at[k])
        )
    weights = [
        pltpu.make_async_copy(w_input_hbm, w_input_ref, weight_sem.at[0]),
        pltpu.make_async_copy(w_hidden_hbm, w_hidden_ref, weight_sem.at[1]),
    ]
    for copy in tables + weights:
        copy.start()

    def clear(step, carry):
        slot_ref[pl.ds(pl.multiple_of(step * 256, 256), 256), :] = jnp.zeros((256, 128), f32)
        return carry

    lax.fori_loop(0, slot_ref.shape[0] // 256, clear, 0)

    def widen(step, carry):
        at = pl.multiple_of(step * 256, 256)
        table_ref[pl.ds(at, 256), :] = half_ref[pl.ds(at, 256), :].astype(f32)
        return carry

    for k in range(4):
        tables[k].wait()
        lax.fori_loop(k * chunk // 256, (k + 1) * chunk // 256, widen, 0)

    def look(sample, carry):
        for slot in range(SLOTS):
            first = sample * LOOK + slot * HOT
            total = table_ref[pl.ds(index_ref[first], 1), :]
            for hot in range(1, HOT):
                total = total + table_ref[pl.ds(index_ref[first + hot], 1), :]
            pooled_ref[pl.ds(slot * samples + sample, 1), :] = total
        return carry

    lax.fori_loop(0, samples, look, 0, unroll=16)

    features = SLOTS * 128
    for slot in range(SLOTS):
        for b in range(BATCHES):
            block = pooled_ref[slot * samples + b * 128 : slot * samples + (b + 1) * 128, :]
            turn_ref[b * features + slot * 128 : b * features + (slot + 1) * 128, :] = jnp.transpose(block)
    turned = jnp.concatenate(
        [
            jnp.concatenate(
                [turn_ref[pl.ds(b * features + s, 16, stride=SHARDS), :] for s in range(SHARDS)],
                axis=0,
            ).astype(bf16)
            for b in range(BATCHES)
        ],
        axis=1,
    )
    pooled = jnp.concatenate(
        [pooled_ref[slot * samples : (slot + 1) * samples, :].astype(bf16) for slot in range(SLOTS)],
        axis=1,
    )
    for copy in weights:
        copy.wait()
    w_input = w_input_ref[...]
    w_hidden = w_hidden_ref[...]
    w_output = w_output_ref[...].astype(f32)
    labels = jnp.concatenate([column(label_ref[b : b + 1, :]) for b in range(BATCHES)], axis=0)
    pre_one = dot(pooled, w_input, ((1,), (0,)))
    act_one = jnp.maximum(pre_one, 0.0).astype(bf16)
    pre_two = dot(act_one, w_hidden, ((1,), (0,)))
    act_two = jnp.maximum(pre_two, 0.0).astype(bf16).astype(f32)
    logits = jnp.sum(act_two * w_output, axis=1, keepdims=True)
    for b in range(BATCHES):
        part = jnp.broadcast_to(logits[b * 128 : (b + 1) * 128], (128, 128))
        logit_ref[b : b + 1, :] = jnp.transpose(part)[0:1, :]
    slope = jax.nn.sigmoid(logits) - labels
    back_two = jnp.where(pre_two > 0, slope * w_output, 0.0).astype(bf16)
    back_one = dot(back_two, w_hidden, ((1,), (1,)))
    back_one = jnp.where(pre_one > 0, back_one, 0.0).astype(bf16)
    back_in = dot(back_one, w_input, ((1,), (1,))).astype(bf16).astype(f32)
    for slot in range(SLOTS):
        pooled_ref[slot * samples : (slot + 1) * samples, :] = back_in[:, slot * 128 : (slot + 1) * 128]
    term_ref[...] = dot(turned, back_one, ((1,), (0,)))

    def scatter(sample, carry):
        for slot in range(SLOTS):
            first = sample * LOOK + slot * HOT
            row = pooled_ref[pl.ds(slot * samples + sample, 1), :]
            for hot in range(HOT):
                slot_ref[pl.ds(place_ref[first + hot], 1), :] = row
        return carry

    lax.fori_loop(0, samples, scatter, 0, unroll=16)

    def pack(owner, carry):
        at = pl.multiple_of(owner * GRAD_ROWS, GRAD_ROWS)
        sent_ref[owner, 0:GRAD_ROWS, :] = slot_ref[pl.ds(at, GRAD_ROWS), :].astype(bf16)
        piece = term_ref[pl.ds(pl.multiple_of(order_ref[owner] * 16, 16), 16), :].astype(bf16)
        for j in range(8):
            sent_ref[owner, GRAD_ROWS + j * 16 : GRAD_ROWS + (j + 1) * 16, :] = piece[
                :, j * 128 : (j + 1) * 128
            ]
        sent_ref[owner, GRAD_ROWS + TERM_ROWS : SENT_ROWS, :] = ids_ref[owner]
        return carry

    step = SHARDS // 4
    stores = []
    for k, target in ((2, sent_hbm), (3, sent_hbm), (0, kept_hbm), (1, kept_hbm)):
        lax.fori_loop(k * step, (k + 1) * step, pack, 0, unroll=4)
        stores.append(
            pltpu.make_async_copy(
                sent_ref.at[pl.ds(k * step, step)],
                target.at[pl.ds((k % 2) * step, step)],
                sent_sem.at[k],
            )
        )
        stores[-1].start()
    for copy in stores:
        copy.wait()


def run_main(index, place, order, own, other, labels, w_input, w_hidden, w_output, ids):
    width = own.shape[1]
    samples = index.shape[0] // LOOK
    smem = pl.BlockSpec(memory_space=pltpu.SMEM)
    vmem = pl.BlockSpec(memory_space=pltpu.VMEM)
    anywhere = pl.BlockSpec(memory_space=pl.ANY)
    return pl.pallas_call(
        main_kernel,
        out_shape=(
            jax.ShapeDtypeStruct((SHARDS // 2, SENT_ROWS, width), bf16),
            jax.ShapeDtypeStruct((SHARDS // 2, SENT_ROWS, width), bf16),
            jax.ShapeDtypeStruct((BATCHES, samples // BATCHES), f32),
        ),
        in_specs=[smem, smem, smem, anywhere, anywhere, vmem, anywhere, anywhere, vmem, vmem],
        out_specs=(anywhere, anywhere, vmem),
        scratch_shapes=[
            pltpu.VMEM((2 * own.shape[0], width), bf16),
            pltpu.VMEM(w_input.shape, bf16),
            pltpu.VMEM(w_hidden.shape, bf16),
            pltpu.VMEM((2 * own.shape[0], width), f32),
            pltpu.VMEM((samples * SLOTS, width), f32),
            pltpu.VMEM((SHARDS * GRAD_ROWS, width), f32),
            pltpu.VMEM((BATCHES * SLOTS * width, samples // BATCHES), f32),
            pltpu.VMEM(w_input.shape, f32),
            pltpu.VMEM((SHARDS, SENT_ROWS, width), bf16),
            pltpu.SemaphoreType.DMA((4,)),
            pltpu.SemaphoreType.DMA((2,)),
            pltpu.SemaphoreType.DMA((4,)),
        ],
        compiler_params=pltpu.CompilerParams(vmem_limit_bytes=40 * 1024 * 1024),
        cost_estimate=pl.CostEstimate(
            flops=2_000_000_000, bytes_accessed=12_000_000, transcendentals=256
        ),
    )(index, place, order, own, other, labels, w_input, w_hidden, w_output, ids)


def owner_kernel(kept_ref, got_ref, out_ref):
    rows = out_ref.shape[1] - TERM_ROWS
    names = lax.broadcasted_iota(jnp.int32, (rows, CAP), 0).astype(f32) + 1.0
    for owner in range(out_ref.shape[0]):
        total = jnp.zeros((rows, out_ref.shape[2]), f32)
        term = jnp.zeros((TERM_ROWS, out_ref.shape[2]), f32)
        for source in (kept_ref, got_ref):
            coded = source[owner, GRAD_ROWS + TERM_ROWS : SENT_ROWS, :].astype(f32)
            picks = []
            for b in range(BATCHES):
                named = coded[b : b + 1] * 256.0 + coded[BATCHES + b : BATCHES + b + 1]
                picks.append(jnp.where(names == named, 1.0, 0.0).astype(bf16))
            pick = jnp.concatenate(picks, axis=1)
            total = total + dot(pick, source[owner, 0:GRAD_ROWS, :], ((1,), (0,)))
            term = term + source[owner, GRAD_ROWS : GRAD_ROWS + TERM_ROWS, :].astype(f32)
        out_ref[owner, 0:rows, :] = total.astype(bf16)
        out_ref[owner, rows : rows + TERM_ROWS, :] = term.astype(bf16)


def run_owner(kept, got, rows):
    owners, _, width = kept.shape
    steps = 8
    block = pl.BlockSpec((owners // steps, SENT_ROWS, width), lambda i: (i, 0, 0))
    return pl.pallas_call(
        owner_kernel,
        grid=(steps,),
        out_shape=jax.ShapeDtypeStruct((owners, rows + TERM_ROWS, width), bf16),
        in_specs=[block, block],
        out_specs=pl.BlockSpec((owners // steps, rows + TERM_ROWS, width), lambda i: (i, 0, 0)),
        compiler_params=pltpu.CompilerParams(vmem_limit_bytes=32 * 1024 * 1024),
        cost_estimate=pl.CostEstimate(
            flops=1_100_000_000, bytes_accessed=6_000_000, transcendentals=0
        ),
    )(kept, got)


def near_kernel(got_ref, out_ref, term_ref):
    rows = got_ref.shape[1] - TERM_ROWS
    part = rows // 4
    for k in range(4):
        total = got_ref[0, k * part : (k + 1) * part, :].astype(f32)
        for source in range(1, 4):
            total = total + got_ref[source, k * part : (k + 1) * part, :].astype(f32)
        out_ref[k, 0:part, :] = total.astype(bf16)
    term = got_ref[0, rows : rows + TERM_ROWS, :].astype(f32)
    for source in range(1, 4):
        term = term + got_ref[source, rows : rows + TERM_ROWS, :].astype(f32)
    term_ref[...] = term
    for k in range(4):
        out_ref[k, part : part + 32, :] = term_ref[pl.ds(k, 32, stride=4), :].astype(bf16)


def run_near(got, rows):
    width = got.shape[2]
    vmem = pl.BlockSpec(memory_space=pltpu.VMEM)
    return pl.pallas_call(
        near_kernel,
        out_shape=jax.ShapeDtypeStruct((4, rows // 4 + 32, width), bf16),
        in_specs=[vmem],
        out_specs=vmem,
        scratch_shapes=[pltpu.VMEM((TERM_ROWS, width), f32)],
        compiler_params=pltpu.CompilerParams(vmem_limit_bytes=32 * 1024 * 1024),
        cost_estimate=pl.CostEstimate(flops=500_000, bytes_accessed=900_000, transcendentals=0),
    )(got)


def owner_order():
    core = lax.axis_index("shard") & 1
    group = jnp.arange(SHARDS, dtype=jnp.int32)
    c = (group >> 4) ^ core
    slow, fast = (group >> 2) & 3, group & 3
    x, y = jnp.where(c == 0, slow, fast), jnp.where(c == 0, fast, slow)
    return x * 8 + y * 2 + c


def group_of(owner):
    core = lax.axis_index("shard") & 1
    x, y, c = owner >> 3, (owner >> 1) & 3, owner & 1
    return (c ^ core) * 16 + jnp.where(c == 0, x * 4 + y, y * 4 + x)


def plan_slots(owner, row):
    batches, samples, looks = owner.shape
    names = jnp.arange(SHARDS, dtype=jnp.int32)
    hit = (owner[..., None] == names).astype(bf16).reshape(batches, samples, looks * SHARDS)
    steps = jnp.arange(samples)
    before = (steps[None, :] < steps[:, None]).astype(bf16)
    rank = jnp.einsum("ts,bsn->btn", before, hit, preferred_element_type=f32)
    counts = jnp.sum(hit.astype(f32), axis=1).reshape(batches, looks, SHARDS)
    turn = jnp.arange(looks)
    base = jnp.sum(
        jnp.where((turn[None, :] < turn[:, None])[None, :, :, None], counts[:, None], 0.0), axis=2
    ).reshape(batches, 1, looks * SHARDS)
    spot = jnp.sum(
        (hit.astype(f32) * (rank + base)).reshape(batches, samples, looks, SHARDS), axis=3
    ).astype(jnp.int32)
    batch = jnp.arange(batches, dtype=jnp.int32)[:, None, None]
    place = owner * GRAD_ROWS + batch * CAP + spot
    code = row + 1
    high = (code >> 8).astype(bf16)
    low = (code & 255).astype(bf16)
    flat_hit = hit.reshape(batches, samples * looks, SHARDS)
    coded = jnp.concatenate(
        [flat_hit * high.reshape(batches, -1, 1), flat_hit * low.reshape(batches, -1, 1)], axis=2
    )
    where = (spot.reshape(batches, -1, 1) == jnp.arange(CAP, dtype=jnp.int32)).astype(bf16)
    ids = jnp.einsum("bin,bip->bnp", coded, where, preferred_element_type=f32).astype(bf16)
    ids = ids.reshape(batches, 2, SHARDS, CAP).transpose(2, 1, 0, 3).reshape(SHARDS, 2 * batches, CAP)
    ids = jnp.pad(ids, ((0, 0), (0, ID_ROWS - 2 * batches), (0, 0)))
    return place.reshape(-1), ids


def table_index(owner, row, rows):
    core = lax.axis_index("shard") & 1
    x, y, c = owner >> 3, (owner >> 1) & 3, owner & 1
    chip = jnp.where(c == 0, y * 4 + x, x * 4 + y)
    return (((c ^ core) * 16 + chip) * rows + row).reshape(-1)


def adagrad_step(table_part, sums_part, grad_part):
    new_sums = sums_part + grad_part * grad_part
    return table_part - learn_rate * grad_part / jnp.sqrt(new_sums)


def local(
    owner_shard, local_row, click_label, row_table, squared_sums, w_input, w_hidden, w_output
):
    rows, width = row_table.shape
    owner = owner_shard[..., 0]
    own, other = gather_table(row_table.astype(bf16))
    index = table_index(owner, local_row, rows)
    place, ids = plan_slots(group_of(owner), local_row)
    kept, sent, logits = run_main(
        index,
        place,
        owner_order(),
        own,
        other,
        click_label.astype(f32),
        w_input,
        w_hidden,
        w_output.reshape(1, -1),
        ids,
    )
    got = lax.ppermute(sent, "shard", SWAP)
    dense = run_owner(kept, got, rows).reshape(4, 4 * (rows + TERM_ROWS), width)
    line = exchange(dense, "shard", FIRST).astype(f32)
    line = jnp.sum(line, axis=0).astype(bf16).reshape(4, rows + TERM_ROWS, width)
    near = exchange(run_near(exchange(line, "shard", SECOND), rows), "grp", NEAR).astype(f32)
    grads = jnp.sum(near[:, 0:128], axis=0).astype(bf16)
    term = jnp.sum(near[:, 128:160], axis=0)
    term = term.reshape(8, 4, width).transpose(1, 0, 2).astype(bf16)
    far = jnp.concatenate([jnp.broadcast_to(grads[None], (4, 128, width)), term], axis=1)
    far = exchange(far, "grp", FAR).astype(f32)
    input_grad = jnp.sum(far[:, 128:136], axis=0).reshape(-1)
    part = jnp.sum(far[:, 0:128], axis=0).astype(bf16)
    total = spread(part, "grp", NEAR).reshape(rows, width).astype(f32)
    new_table = adagrad_step(row_table, squared_sums, total)
    return (new_table, logits, input_grad)


def solution(mesh):
    in_specs = (
        P(None, ("grp", "shard"), None, None),
        P(None, ("grp", "shard"), None),
        P(None, ("grp", "shard")),
        P("shard", None),
        P("shard", None),
        P(),
        P(),
        P(),
    )
    out_specs = (P("shard", None), P(None, ("grp", "shard")), P(("grp", "shard")))
    return jax.shard_map(local, mesh=mesh, in_specs=in_specs, out_specs=out_specs, check_vma=False)
```

```python
import jax
import jax.numpy as jnp
from jax import lax
from jax.experimental import pallas as pl
from jax.experimental.pallas import tpu as pltpu
from jax.sharding import PartitionSpec as P

bf16 = jnp.bfloat16
f32 = jnp.float32
learn_rate = 0.1

SLOTS = 4
HOT = 4
LOOK = 16
SHARDS = 32
CAP = 128
BATCHES = 2
GRAD_ROWS = BATCHES * CAP
TERM_ROWS = 128
ID_ROWS = 16
SENT_ROWS = GRAD_ROWS + TERM_ROWS + ID_ROWS

FIRST = [[x * 8 + y * 2 for x in range(4)] for y in range(4)] + [
    [x * 8 + y * 2 + 1 for y in range(4)] for x in range(4)
]
SECOND = [[x * 8 + y * 2 for y in range(4)] for x in range(4)] + [
    [x * 8 + y * 2 + 1 for x in range(4)] for y in range(4)
]
SWAP = [(i, i ^ 1) for i in range(SHARDS)]
NEAR = [[4 * i + j for j in range(4)] for i in range(4)]
FAR = [[4 * i + j for i in range(4)] for j in range(4)]


def exchange(value, axis, groups=None):
    return lax.all_to_all(
        value, axis, split_axis=0, concat_axis=0, tiled=True, axis_index_groups=groups
    )


def spread(value, axis, groups):
    return exchange(jnp.broadcast_to(value[None], (4,) + value.shape), axis, groups)


def dot(a, b, dims):
    return lax.dot_general(a, b, (dims, ((), ())), preferred_element_type=f32)


def column(row):
    return jnp.transpose(jnp.broadcast_to(row, (128, 128)))[:, 0:1]


def main_kernel(
    index_ref,
    place_ref,
    order_ref,
    own_hbm,
    other_hbm,
    label_ref,
    w_input_hbm,
    w_hidden_hbm,
    w_output_ref,
    ids_ref,
    kept_hbm,
    sent_hbm,
    logit_ref,
    half_ref,
    w_input_ref,
    w_hidden_ref,
    table_ref,
    pooled_ref,
    slot_ref,
    turn_ref,
    turned_ref,
    back_ref,
    term_ref,
    sent_ref,
    half_sem,
    weight_sem,
    sent_sem,
):
    half = own_hbm.shape[0]
    chunk = half // 2
    samples = pooled_ref.shape[0] // SLOTS
    tables = []
    for k in range(4):
        source = (own_hbm, other_hbm)[k // 2].at[pl.ds((k % 2) * chunk, chunk)]
        tables.append(
            pltpu.make_async_copy(source, half_ref.at[pl.ds(k * chunk, chunk)], half_sem.at[k])
        )
    weights = [
        pltpu.make_async_copy(w_input_hbm, w_input_ref, weight_sem.at[0]),
        pltpu.make_async_copy(w_hidden_hbm, w_hidden_ref, weight_sem.at[1]),
    ]
    for copy in tables + weights:
        copy.start()

    def widen(step, carry):
        at = pl.multiple_of(step * 256, 256)
        table_ref[pl.ds(at, 256), :] = half_ref[pl.ds(at, 256), :].astype(f32)
        return carry

    for k in range(4):
        tables[k].wait()
        lax.fori_loop(k * chunk // 256, (k + 1) * chunk // 256, widen, 0)

    def look(step, carry):
        slot_ref[pl.ds(pl.multiple_of(step * 512, 512), 512), :] = jnp.zeros((512, 128), f32)
        for turn in range(16):
            sample = step * 16 + turn
            for slot in range(SLOTS):
                first = sample * LOOK + slot * HOT
                total = table_ref[pl.ds(index_ref[first], 1), :]
                for hot in range(1, HOT):
                    total = total + table_ref[pl.ds(index_ref[first + hot], 1), :]
                pooled_ref[pl.ds(slot * samples + sample, 1), :] = total
        return carry

    lax.fori_loop(0, samples // 16, look, 0)

    features = SLOTS * 128
    for slot in range(SLOTS):
        for b in range(BATCHES):
            block = pooled_ref[slot * samples + b * 128 : slot * samples + (b + 1) * 128, :]
            turn_ref[b * features + slot * 128 : b * features + (slot + 1) * 128, :] = jnp.transpose(block)
    turned_ref[...] = jnp.concatenate(
        [
            jnp.concatenate(
                [turn_ref[pl.ds(b * features + s, 16, stride=SHARDS), :] for s in range(SHARDS)],
                axis=0,
            ).astype(bf16)
            for b in range(BATCHES)
        ],
        axis=1,
    )
    pooled = jnp.concatenate(
        [pooled_ref[slot * samples : (slot + 1) * samples, :].astype(bf16) for slot in range(SLOTS)],
        axis=1,
    )
    for copy in weights:
        copy.wait()
    w_input = w_input_ref[...]
    w_hidden = w_hidden_ref[...]
    w_output = w_output_ref[...].astype(f32)
    labels = jnp.concatenate([column(label_ref[b : b + 1, :]) for b in range(BATCHES)], axis=0)
    pre_one = dot(pooled, w_input, ((1,), (0,)))
    act_one = jnp.maximum(pre_one, 0.0).astype(bf16)
    pre_two = dot(act_one, w_hidden, ((1,), (0,)))
    act_two = jnp.maximum(pre_two, 0.0).astype(bf16).astype(f32)
    logits = jnp.sum(act_two * w_output, axis=1, keepdims=True)
    for b in range(BATCHES):
        part = jnp.broadcast_to(logits[b * 128 : (b + 1) * 128], (128, 128))
        logit_ref[b : b + 1, :] = jnp.transpose(part)[0:1, :]
    slope = jax.nn.sigmoid(logits) - labels
    back_two = jnp.where(pre_two > 0, slope * w_output, 0.0).astype(bf16)
    back_one = dot(back_two, w_hidden, ((1,), (1,)))
    back_one = jnp.where(pre_one > 0, back_one, 0.0).astype(bf16)
    back_in = dot(back_one, w_input, ((1,), (1,))).astype(bf16).astype(f32)
    for slot in range(SLOTS):
        pooled_ref[slot * samples : (slot + 1) * samples, :] = back_in[:, slot * 128 : (slot + 1) * 128]
    for j in range(8):
        back_ref[j] = back_one[:, j * 128 : (j + 1) * 128]

    def scatter(step, carry):
        term_ref[step] = dot(turned_ref[...], back_ref[step], ((1,), (0,)))
        for turn in range(32):
            sample = step * 32 + turn
            for slot in range(SLOTS):
                first = sample * LOOK + slot * HOT
                row = pooled_ref[pl.ds(slot * samples + sample, 1), :]
                for hot in range(HOT):
                    slot_ref[pl.ds(place_ref[first + hot], 1), :] = row
        return carry

    lax.fori_loop(0, samples // 32, scatter, 0)

    def pack(owner, carry):
        at = pl.multiple_of(owner * GRAD_ROWS, GRAD_ROWS)
        sent_ref[owner, 0:GRAD_ROWS, :] = slot_ref[pl.ds(at, GRAD_ROWS), :].astype(bf16)
        piece = pl.ds(pl.multiple_of(order_ref[owner] * 16, 16), 16)
        for j in range(8):
            sent_ref[owner, GRAD_ROWS + j * 16 : GRAD_ROWS + (j + 1) * 16, :] = term_ref[
                j, piece, :
            ].astype(bf16)
        sent_ref[owner, GRAD_ROWS + TERM_ROWS : SENT_ROWS, :] = ids_ref[owner]
        return carry

    step = SHARDS // 4
    stores = []
    for k, target in ((2, sent_hbm), (3, sent_hbm), (0, kept_hbm), (1, kept_hbm)):
        lax.fori_loop(k * step, (k + 1) * step, pack, 0, unroll=4)
        stores.append(
            pltpu.make_async_copy(
                sent_ref.at[pl.ds(k * step, step)],
                target.at[pl.ds((k % 2) * step, step)],
                sent_sem.at[k],
            )
        )
        stores[-1].start()
    for copy in stores:
        copy.wait()


def run_main(index, place, order, own, other, labels, w_input, w_hidden, w_output, ids):
    width = own.shape[1]
    samples = index.shape[0] // LOOK
    smem = pl.BlockSpec(memory_space=pltpu.SMEM)
    vmem = pl.BlockSpec(memory_space=pltpu.VMEM)
    anywhere = pl.BlockSpec(memory_space=pl.ANY)
    hbm = pl.BlockSpec(memory_space=pltpu.HBM)
    return pl.pallas_call(
        main_kernel,
        out_shape=(
            jax.ShapeDtypeStruct((SHARDS // 2, SENT_ROWS, width), bf16),
            jax.ShapeDtypeStruct((SHARDS // 2, SENT_ROWS, width), bf16),
            jax.ShapeDtypeStruct((BATCHES, samples // BATCHES), f32),
        ),
        in_specs=[smem, smem, smem, anywhere, anywhere, vmem, hbm, hbm, vmem, vmem],
        out_specs=(anywhere, anywhere, vmem),
        scratch_shapes=[
            pltpu.VMEM((2 * own.shape[0], width), bf16),
            pltpu.VMEM(w_input.shape, bf16),
            pltpu.VMEM(w_hidden.shape, bf16),
            pltpu.VMEM((2 * own.shape[0], width), f32),
            pltpu.VMEM((samples * SLOTS, width), f32),
            pltpu.VMEM((SHARDS * GRAD_ROWS, width), f32),
            pltpu.VMEM((BATCHES * SLOTS * width, samples // BATCHES), f32),
            pltpu.VMEM((SLOTS * width, samples), bf16),
            pltpu.VMEM((8, samples, width), bf16),
            pltpu.VMEM((8, SLOTS * width, width), f32),
            pltpu.VMEM((SHARDS, SENT_ROWS, width), bf16),
            pltpu.SemaphoreType.DMA((4,)),
            pltpu.SemaphoreType.DMA((2,)),
            pltpu.SemaphoreType.DMA((4,)),
        ],
        compiler_params=pltpu.CompilerParams(vmem_limit_bytes=40 * 1024 * 1024),
        cost_estimate=pl.CostEstimate(
            flops=2_000_000_000, bytes_accessed=12_000_000, transcendentals=256
        ),
    )(index, place, order, own, other, labels, w_input, w_hidden, w_output, ids)


def add_source(source, owner, total, term):
    names = lax.broadcasted_iota(jnp.int32, (total.shape[0], CAP), 0).astype(f32) + 1.0
    coded = source[owner, GRAD_ROWS + TERM_ROWS : SENT_ROWS, :].astype(f32)
    picks = []
    for b in range(BATCHES):
        named = coded[b : b + 1] * 256.0 + coded[BATCHES + b : BATCHES + b + 1]
        picks.append(jnp.where(names == named, 1.0, 0.0).astype(bf16))
    pick = jnp.concatenate(picks, axis=1)
    total = total + dot(pick, source[owner, 0:GRAD_ROWS, :], ((1,), (0,)))
    return total, term + source[owner, GRAD_ROWS : GRAD_ROWS + TERM_ROWS, :].astype(f32)


def kept_kernel(kept_ref, out_ref):
    rows = out_ref.shape[1] - TERM_ROWS
    width = out_ref.shape[2]
    for owner in range(out_ref.shape[0]):
        total = jnp.zeros((rows, width), f32)
        term = jnp.zeros((TERM_ROWS, width), f32)
        total, term = add_source(kept_ref, owner, total, term)
        out_ref[owner, 0:rows, :] = total.astype(bf16)
        out_ref[owner, rows : rows + TERM_ROWS, :] = term.astype(bf16)


def got_kernel(base_ref, got_ref, out_ref):
    rows = out_ref.shape[1] - TERM_ROWS
    for owner in range(out_ref.shape[0]):
        total = base_ref[owner, 0:rows, :].astype(f32)
        term = base_ref[owner, rows : rows + TERM_ROWS, :].astype(f32)
        total, term = add_source(got_ref, owner, total, term)
        out_ref[owner, 0:rows, :] = total.astype(bf16)
        out_ref[owner, rows : rows + TERM_ROWS, :] = term.astype(bf16)


def run_owner(kernel, rows, *operands):
    owners, _, width = operands[0].shape
    steps = 8
    blocks = [
        pl.BlockSpec((owners // steps, each.shape[1], width), lambda i: (i, 0, 0))
        for each in operands
    ]
    return pl.pallas_call(
        kernel,
        grid=(steps,),
        out_shape=jax.ShapeDtypeStruct((owners, rows + TERM_ROWS, width), bf16),
        in_specs=blocks,
        out_specs=pl.BlockSpec((owners // steps, rows + TERM_ROWS, width), lambda i: (i, 0, 0)),
        compiler_params=pltpu.CompilerParams(vmem_limit_bytes=32 * 1024 * 1024),
        cost_estimate=pl.CostEstimate(
            flops=550_000_000, bytes_accessed=5_000_000, transcendentals=0
        ),
    )(*operands)


def near_kernel(got_ref, out_ref, term_ref):
    rows = got_ref.shape[1] - TERM_ROWS
    part = rows // 4
    for k in range(4):
        total = got_ref[0, k * part : (k + 1) * part, :].astype(f32)
        for source in range(1, 4):
            total = total + got_ref[source, k * part : (k + 1) * part, :].astype(f32)
        out_ref[k, 0:part, :] = total.astype(bf16)
    term = got_ref[0, rows : rows + TERM_ROWS, :].astype(f32)
    for source in range(1, 4):
        term = term + got_ref[source, rows : rows + TERM_ROWS, :].astype(f32)
    term_ref[...] = term
    for k in range(4):
        out_ref[k, part : part + 32, :] = term_ref[pl.ds(k, 32, stride=4), :].astype(bf16)


def run_near(got, rows):
    width = got.shape[2]
    vmem = pl.BlockSpec(memory_space=pltpu.VMEM)
    return pl.pallas_call(
        near_kernel,
        out_shape=jax.ShapeDtypeStruct((4, rows // 4 + 32, width), bf16),
        in_specs=[vmem],
        out_specs=vmem,
        scratch_shapes=[pltpu.VMEM((TERM_ROWS, width), f32)],
        compiler_params=pltpu.CompilerParams(vmem_limit_bytes=32 * 1024 * 1024),
        cost_estimate=pl.CostEstimate(flops=500_000, bytes_accessed=900_000, transcendentals=0),
    )(got)


def owner_order(core):
    group = jnp.arange(SHARDS, dtype=jnp.int32)
    c = (group >> 4) ^ core
    slow, fast = (group >> 2) & 3, group & 3
    x, y = jnp.where(c == 0, slow, fast), jnp.where(c == 0, fast, slow)
    return x * 8 + y * 2 + c


def group_of(owner, core):
    x, y, c = owner >> 3, (owner >> 1) & 3, owner & 1
    return (c ^ core) * 16 + jnp.where(c == 0, x * 4 + y, y * 4 + x)


def plan_slots(owner, row, after):
    batches, samples, looks = owner.shape
    names, steps, turn, batch, spots, after = lax.optimization_barrier(
        (
            jnp.arange(SHARDS, dtype=jnp.int32),
            jnp.arange(samples),
            jnp.arange(looks),
            jnp.arange(batches, dtype=jnp.int32),
            jnp.arange(CAP, dtype=jnp.int32),
            after,
        )
    )
    hit = (owner[..., None] == names).astype(bf16).reshape(batches, samples, looks * SHARDS)
    before = (steps[None, :] < steps[:, None]).astype(bf16)
    rank = jnp.einsum("ts,bsn->btn", before, hit, preferred_element_type=f32)
    counts = jnp.sum(hit.astype(f32), axis=1).reshape(batches, looks, SHARDS)
    base = jnp.sum(
        jnp.where((turn[None, :] < turn[:, None])[None, :, :, None], counts[:, None], 0.0), axis=2
    ).reshape(batches, 1, looks * SHARDS)
    spot = jnp.sum(
        (hit.astype(f32) * (rank + base)).reshape(batches, samples, looks, SHARDS), axis=3
    ).astype(jnp.int32)
    place = owner * GRAD_ROWS + batch[:, None, None] * CAP + spot
    code = row + 1
    high = (code >> 8).astype(bf16)
    low = (code & 255).astype(bf16)
    flat_hit = hit.reshape(batches, samples * looks, SHARDS)
    coded = jnp.concatenate(
        [flat_hit * high.reshape(batches, -1, 1), flat_hit * low.reshape(batches, -1, 1)], axis=2
    )
    where = (spot.reshape(batches, -1, 1) == spots).astype(bf16)
    ids = jnp.einsum("bin,bip->bnp", coded, where, preferred_element_type=f32).astype(bf16)
    ids = ids.reshape(batches, 2, SHARDS, CAP).transpose(2, 1, 0, 3).reshape(SHARDS, 2 * batches, CAP)
    ids = jnp.pad(ids, ((0, 0), (0, ID_ROWS - 2 * batches), (0, 0)))
    return place.reshape(-1), ids


def table_index(owner, row, rows, core):
    x, y, c = owner >> 3, (owner >> 1) & 3, owner & 1
    chip = jnp.where(c == 0, y * 4 + x, x * 4 + y)
    return (((c ^ core) * 16 + chip) * rows + row).reshape(-1)


def adagrad_step(table_part, sums_part, grad_part):
    new_sums = sums_part + grad_part * grad_part
    return table_part - learn_rate * grad_part / jnp.sqrt(new_sums)


def local(
    owner_shard, local_row, click_label, row_table, squared_sums, w_input, w_hidden, w_output
):
    rows, width = row_table.shape
    owner = owner_shard[..., 0]
    core = lax.axis_index("shard") & 1
    table_low, core = lax.optimization_barrier((row_table.astype(bf16), core))
    line = spread(table_low, "shard", FIRST).reshape(4 * rows, width)
    own = spread(line, "shard", SECOND).reshape(16 * rows, width)
    own, owner, local_row, click_label, core = lax.optimization_barrier(
        (own, owner, local_row, click_label, core)
    )
    other = lax.ppermute(own, "shard", SWAP)
    index = table_index(owner, local_row, rows, core)
    order = owner_order(core)
    place, ids = plan_slots(group_of(owner, core), local_row, own)
    labels = click_label.astype(f32)
    kept, sent, logits = run_main(
        index,
        place,
        order,
        own,
        other,
        labels,
        w_input,
        w_hidden,
        w_output.reshape(1, -1),
        ids,
    )
    got = lax.ppermute(sent, "shard", SWAP)
    dense = run_owner(got_kernel, rows, run_owner(kept_kernel, rows, kept), got)
    dense = dense.reshape(4, 4 * (rows + TERM_ROWS), width)
    line = exchange(dense, "shard", FIRST).astype(f32)
    line = jnp.sum(line, axis=0).astype(bf16).reshape(4, rows + TERM_ROWS, width)
    near = exchange(run_near(exchange(line, "shard", SECOND), rows), "grp", NEAR).astype(f32)
    grads = jnp.sum(near[:, 0:128], axis=0).astype(bf16)
    term = jnp.sum(near[:, 128:160], axis=0)
    term = term.reshape(8, 4, width).transpose(1, 0, 2).astype(bf16)
    far = jnp.concatenate([jnp.broadcast_to(grads[None], (4, 128, width)), term], axis=1)
    far = exchange(far, "grp", FAR).astype(f32)
    input_grad = jnp.sum(far[:, 128:136], axis=0).reshape(-1)
    part = jnp.sum(far[:, 0:128], axis=0).astype(bf16)
    part, input_grad = lax.optimization_barrier((part, input_grad))
    total = spread(part, "grp", NEAR).reshape(rows, width).astype(f32)
    new_table = adagrad_step(row_table, squared_sums, total)
    return (new_table, logits, input_grad)


def solution(mesh):
    in_specs = (
        P(None, ("grp", "shard"), None, None),
        P(None, ("grp", "shard"), None),
        P(None, ("grp", "shard")),
        P("shard", None),
        P("shard", None),
        P(),
        P(),
        P(),
    )
    out_specs = (P("shard", None), P(None, ("grp", "shard")), P(("grp", "shard")))
    return jax.shard_map(local, mesh=mesh, in_specs=in_specs, out_specs=out_specs, check_vma=False)
```

```python
import jax
import jax.numpy as jnp
from jax import lax
from jax.experimental import pallas as pl
from jax.experimental.pallas import tpu as pltpu
from jax.sharding import PartitionSpec as P

bf16 = jnp.bfloat16
f32 = jnp.float32
learn_rate = 0.1

SLOTS = 4
HOT = 4
LOOK = 16
SHARDS = 32
CAP = 128
BATCHES = 2
GRAD_ROWS = BATCHES * CAP
TERM_ROWS = 128
ID_ROWS = 16
SENT_ROWS = GRAD_ROWS + TERM_ROWS + ID_ROWS

FIRST = [[x * 8 + y * 2 for x in range(4)] for y in range(4)] + [
    [x * 8 + y * 2 + 1 for y in range(4)] for x in range(4)
]
SECOND = [[x * 8 + y * 2 for y in range(4)] for x in range(4)] + [
    [x * 8 + y * 2 + 1 for x in range(4)] for y in range(4)
]
SWAP = [(i, i ^ 1) for i in range(SHARDS)]
NEAR = [[4 * i + j for j in range(4)] for i in range(4)]
FAR = [[4 * i + j for i in range(4)] for j in range(4)]


def exchange(value, axis, groups=None):
    return lax.all_to_all(
        value, axis, split_axis=0, concat_axis=0, tiled=True, axis_index_groups=groups
    )


def spread(value, axis, groups):
    return exchange(jnp.broadcast_to(value[None], (4,) + value.shape), axis, groups)


def dot(a, b, dims):
    return lax.dot_general(a, b, (dims, ((), ())), preferred_element_type=f32)


def column(row):
    return jnp.transpose(jnp.broadcast_to(row, (128, 128)))[:, 0:1]


def main_kernel(
    index_ref,
    place_ref,
    order_ref,
    own_ref,
    other_ref,
    label_ref,
    w_input_ref,
    w_hidden_ref,
    w_output_ref,
    ids_ref,
    kept_ref,
    sent_ref,
    logit_ref,
    table_ref,
    pooled_ref,
    slot_ref,
    turn_ref,
    turned_ref,
    back_ref,
    term_ref,
):
    half = own_ref.shape[0]
    samples = pooled_ref.shape[0] // SLOTS

    def widen(step, carry):
        at = pl.multiple_of(step * 256, 256)
        table_ref[pl.ds(at, 256), :] = own_ref[pl.ds(at, 256), :].astype(f32)
        table_ref[pl.ds(half + at, 256), :] = other_ref[pl.ds(at, 256), :].astype(f32)
        return carry

    lax.fori_loop(0, half // 256, widen, 0)

    def look(step, carry):
        slot_ref[pl.ds(pl.multiple_of(step * 512, 512), 512), :] = jnp.zeros((512, 128), f32)
        for turn in range(16):
            sample = step * 16 + turn
            for slot in range(SLOTS):
                first = sample * LOOK + slot * HOT
                total = table_ref[pl.ds(index_ref[first], 1), :]
                for hot in range(1, HOT):
                    total = total + table_ref[pl.ds(index_ref[first + hot], 1), :]
                pooled_ref[pl.ds(slot * samples + sample, 1), :] = total
        return carry

    lax.fori_loop(0, samples // 16, look, 0)

    features = SLOTS * 128
    for slot in range(SLOTS):
        for b in range(BATCHES):
            block = pooled_ref[slot * samples + b * 128 : slot * samples + (b + 1) * 128, :]
            turn_ref[b * features + slot * 128 : b * features + (slot + 1) * 128, :] = jnp.transpose(block)
    turned_ref[...] = jnp.concatenate(
        [
            jnp.concatenate(
                [turn_ref[pl.ds(b * features + s, 16, stride=SHARDS), :] for s in range(SHARDS)],
                axis=0,
            ).astype(bf16)
            for b in range(BATCHES)
        ],
        axis=1,
    )
    pooled = jnp.concatenate(
        [pooled_ref[slot * samples : (slot + 1) * samples, :].astype(bf16) for slot in range(SLOTS)],
        axis=1,
    )
    w_input = w_input_ref[...]
    w_hidden = w_hidden_ref[...]
    w_output = w_output_ref[...].astype(f32)
    labels = jnp.concatenate([column(label_ref[b : b + 1, :]) for b in range(BATCHES)], axis=0)
    pre_one = dot(pooled, w_input, ((1,), (0,)))
    act_one = jnp.maximum(pre_one, 0.0).astype(bf16)
    pre_two = dot(act_one, w_hidden, ((1,), (0,)))
    act_two = jnp.maximum(pre_two, 0.0).astype(bf16).astype(f32)
    logits = jnp.sum(act_two * w_output, axis=1, keepdims=True)
    for b in range(BATCHES):
        part = jnp.broadcast_to(logits[b * 128 : (b + 1) * 128], (128, 128))
        logit_ref[b : b + 1, :] = jnp.transpose(part)[0:1, :]
    slope = jax.nn.sigmoid(logits) - labels
    back_two = jnp.where(pre_two > 0, slope * w_output, 0.0).astype(bf16)
    back_one = dot(back_two, w_hidden, ((1,), (1,)))
    back_one = jnp.where(pre_one > 0, back_one, 0.0).astype(bf16)
    back_in = dot(back_one, w_input, ((1,), (1,))).astype(bf16).astype(f32)
    for slot in range(SLOTS):
        pooled_ref[slot * samples : (slot + 1) * samples, :] = back_in[:, slot * 128 : (slot + 1) * 128]
    for j in range(8):
        back_ref[j] = back_one[:, j * 128 : (j + 1) * 128]

    def scatter(step, carry):
        term_ref[step] = dot(turned_ref[...], back_ref[step], ((1,), (0,)))
        for turn in range(32):
            sample = step * 32 + turn
            for slot in range(SLOTS):
                first = sample * LOOK + slot * HOT
                row = pooled_ref[pl.ds(slot * samples + sample, 1), :]
                for hot in range(HOT):
                    slot_ref[pl.ds(place_ref[first + hot], 1), :] = row
        return carry

    lax.fori_loop(0, samples // 32, scatter, 0)

    for target, base in ((sent_ref, SHARDS // 2), (kept_ref, 0)):

        def pack(owner, carry):
            at = pl.multiple_of((base + owner) * GRAD_ROWS, GRAD_ROWS)
            target[owner, 0:GRAD_ROWS, :] = slot_ref[pl.ds(at, GRAD_ROWS), :].astype(bf16)
            piece = pl.ds(pl.multiple_of(order_ref[base + owner] * 16, 16), 16)
            for j in range(8):
                target[owner, GRAD_ROWS + j * 16 : GRAD_ROWS + (j + 1) * 16, :] = term_ref[
                    j, piece, :
                ].astype(bf16)
            target[owner, GRAD_ROWS + TERM_ROWS : SENT_ROWS, :] = ids_ref[base + owner]
            return carry

        lax.fori_loop(0, SHARDS // 2, pack, 0, unroll=4)


def run_main(index, place, order, own, other, labels, w_input, w_hidden, w_output, ids):
    width = own.shape[1]
    samples = index.shape[0] // LOOK
    smem = pl.BlockSpec(memory_space=pltpu.SMEM)
    vmem = pl.BlockSpec(memory_space=pltpu.VMEM)
    return pl.pallas_call(
        main_kernel,
        out_shape=(
            jax.ShapeDtypeStruct((SHARDS // 2, SENT_ROWS, width), bf16),
            jax.ShapeDtypeStruct((SHARDS // 2, SENT_ROWS, width), bf16),
            jax.ShapeDtypeStruct((BATCHES, samples // BATCHES), f32),
        ),
        in_specs=[smem] * 3 + [vmem] * 7,
        out_specs=(vmem, vmem, vmem),
        scratch_shapes=[
            pltpu.VMEM((2 * own.shape[0], width), f32),
            pltpu.VMEM((samples * SLOTS, width), f32),
            pltpu.VMEM((SHARDS * GRAD_ROWS, width), f32),
            pltpu.VMEM((BATCHES * SLOTS * width, samples // BATCHES), f32),
            pltpu.VMEM((SLOTS * width, samples), bf16),
            pltpu.VMEM((8, samples, width), bf16),
            pltpu.VMEM((8, SLOTS * width, width), f32),
        ],
        compiler_params=pltpu.CompilerParams(vmem_limit_bytes=40 * 1024 * 1024),
        cost_estimate=pl.CostEstimate(
            flops=2_000_000_000, bytes_accessed=12_000_000, transcendentals=256
        ),
    )(index, place, order, own, other, labels, w_input, w_hidden, w_output, ids)


def row_code(row):
    return jnp.where(row < 256, row + 1, 255 - row).astype(f32).astype(bf16)


def add_source(source, owner, total, term):
    rows = lax.broadcasted_iota(jnp.int32, (total.shape[0], CAP), 0)
    names = row_code(rows)
    coded = source[owner, GRAD_ROWS + TERM_ROWS : SENT_ROWS, :]
    one, zero = jnp.ones((), bf16), jnp.zeros((), bf16)
    pick = jnp.concatenate(
        [jnp.where(names == coded[b : b + 1], one, zero) for b in range(BATCHES)], axis=1
    )
    total = total + dot(pick, source[owner, 0:GRAD_ROWS, :], ((1,), (0,)))
    return total, term + source[owner, GRAD_ROWS : GRAD_ROWS + TERM_ROWS, :].astype(f32)


def kept_kernel(kept_ref, out_ref):
    rows = out_ref.shape[1] - TERM_ROWS
    width = out_ref.shape[2]

    def step(owner, carry):
        total = jnp.zeros((rows, width), f32)
        term = jnp.zeros((TERM_ROWS, width), f32)
        total, term = add_source(kept_ref, owner, total, term)
        out_ref[owner, 0:rows, :] = total.astype(bf16)
        out_ref[owner, rows : rows + TERM_ROWS, :] = term.astype(bf16)
        return carry

    lax.fori_loop(0, out_ref.shape[0], step, 0, unroll=2)


def got_kernel(base_ref, got_ref, out_ref):
    rows = out_ref.shape[1] - TERM_ROWS

    def step(owner, carry):
        total = base_ref[owner, 0:rows, :].astype(f32)
        term = base_ref[owner, rows : rows + TERM_ROWS, :].astype(f32)
        total, term = add_source(got_ref, owner, total, term)
        out_ref[owner, 0:rows, :] = total.astype(bf16)
        out_ref[owner, rows : rows + TERM_ROWS, :] = term.astype(bf16)
        return carry

    lax.fori_loop(0, out_ref.shape[0], step, 0, unroll=2)


def run_owner(kernel, rows, *operands):
    owners, _, width = operands[0].shape
    vmem = pl.BlockSpec(memory_space=pltpu.VMEM)
    return pl.pallas_call(
        kernel,
        out_shape=jax.ShapeDtypeStruct((owners, rows + TERM_ROWS, width), bf16),
        in_specs=[vmem] * len(operands),
        out_specs=vmem,
        compiler_params=pltpu.CompilerParams(vmem_limit_bytes=32 * 1024 * 1024),
        cost_estimate=pl.CostEstimate(
            flops=550_000_000, bytes_accessed=5_000_000, transcendentals=0
        ),
    )(*operands)


def near_kernel(got_ref, out_ref, term_ref):
    rows = got_ref.shape[1] - TERM_ROWS
    part = rows // 4
    for k in range(4):
        total = got_ref[0, k * part : (k + 1) * part, :].astype(f32)
        for source in range(1, 4):
            total = total + got_ref[source, k * part : (k + 1) * part, :].astype(f32)
        out_ref[k, 0:part, :] = total.astype(bf16)
    term = got_ref[0, rows : rows + TERM_ROWS, :].astype(f32)
    for source in range(1, 4):
        term = term + got_ref[source, rows : rows + TERM_ROWS, :].astype(f32)
    term_ref[...] = term
    for k in range(4):
        out_ref[k, part : part + 32, :] = term_ref[pl.ds(k, 32, stride=4), :].astype(bf16)


def run_near(got, rows):
    width = got.shape[2]
    vmem = pl.BlockSpec(memory_space=pltpu.VMEM)
    return pl.pallas_call(
        near_kernel,
        out_shape=jax.ShapeDtypeStruct((4, rows // 4 + 32, width), bf16),
        in_specs=[vmem],
        out_specs=vmem,
        scratch_shapes=[pltpu.VMEM((TERM_ROWS, width), f32)],
        compiler_params=pltpu.CompilerParams(vmem_limit_bytes=32 * 1024 * 1024),
        cost_estimate=pl.CostEstimate(flops=500_000, bytes_accessed=900_000, transcendentals=0),
    )(got)


def sum_of(got_ref, first, last):
    total = got_ref[0, first:last].astype(f32)
    for source in range(1, 4):
        total = total + got_ref[source, first:last].astype(f32)
    return total


def far_kernel(got_ref, out_ref):
    total = sum_of(got_ref, 0, out_ref.shape[1]).astype(bf16)
    for k in range(4):
        out_ref[k] = total


def run_far(got):
    _, rows, width = got.shape
    vmem = pl.BlockSpec(memory_space=pltpu.VMEM)
    return pl.pallas_call(
        far_kernel,
        out_shape=jax.ShapeDtypeStruct((4, rows - 8, width), bf16),
        in_specs=[vmem],
        out_specs=vmem,
        compiler_params=pltpu.CompilerParams(vmem_limit_bytes=16 * 1024 * 1024),
        cost_estimate=pl.CostEstimate(flops=70_000, bytes_accessed=300_000, transcendentals=0),
    )(got)


def final_kernel(total_ref, table_ref, sums_ref, got_ref, new_ref, term_ref):
    grad = total_ref[...].astype(f32)
    new_sums = sums_ref[...] + grad * grad
    new_ref[...] = table_ref[...] - learn_rate * grad / jnp.sqrt(new_sums)
    term_ref[...] = sum_of(got_ref, got_ref.shape[1] - 8, got_ref.shape[1])


def run_final(total, table, sums, got):
    vmem = pl.BlockSpec(memory_space=pltpu.VMEM)
    return pl.pallas_call(
        final_kernel,
        out_shape=(
            jax.ShapeDtypeStruct(table.shape, f32),
            jax.ShapeDtypeStruct((8, table.shape[1]), f32),
        ),
        in_specs=[vmem] * 4,
        out_specs=(vmem, vmem),
        compiler_params=pltpu.CompilerParams(vmem_limit_bytes=16 * 1024 * 1024),
        cost_estimate=pl.CostEstimate(
            flops=500_000, bytes_accessed=1_000_000, transcendentals=65536
        ),
    )(total, table, sums, got)


def owner_order(core):
    group = jnp.arange(SHARDS, dtype=jnp.int32)
    c = (group >> 4) ^ core
    slow, fast = (group >> 2) & 3, group & 3
    x, y = jnp.where(c == 0, slow, fast), jnp.where(c == 0, fast, slow)
    return x * 8 + y * 2 + c


def group_of(owner, core):
    x, y, c = owner >> 3, (owner >> 1) & 3, owner & 1
    return (c ^ core) * 16 + jnp.where(c == 0, x * 4 + y, y * 4 + x)


def plan_slots(owner, row, after):
    batches, samples, looks = owner.shape
    names, steps, turn, batch, spots, after = lax.optimization_barrier(
        (
            jnp.arange(SHARDS, dtype=jnp.int32),
            jnp.arange(samples),
            jnp.arange(looks),
            jnp.arange(batches, dtype=jnp.int32),
            jnp.arange(CAP, dtype=jnp.int32),
            after,
        )
    )
    hit = (owner[..., None] == names).astype(bf16).reshape(batches, samples, looks * SHARDS)
    before = (steps[None, :] < steps[:, None]).astype(bf16)
    rank = jnp.einsum("ts,bsn->btn", before, hit, preferred_element_type=f32)
    counts = jnp.sum(hit.astype(f32), axis=1).reshape(batches, looks, SHARDS)
    base = jnp.sum(
        jnp.where((turn[None, :] < turn[:, None])[None, :, :, None], counts[:, None], 0.0), axis=2
    ).reshape(batches, 1, looks * SHARDS)
    spot = jnp.sum(
        (hit.astype(f32) * (rank + base)).reshape(batches, samples, looks, SHARDS), axis=3
    ).astype(jnp.int32)
    place = owner * GRAD_ROWS + batch[:, None, None] * CAP + spot
    flat_hit = hit.reshape(batches, samples * looks, SHARDS)
    coded = flat_hit * row_code(row).reshape(batches, -1, 1)
    where = (spot.reshape(batches, -1, 1) == spots).astype(bf16)
    ids = jnp.einsum("bin,bip->bnp", coded, where, preferred_element_type=f32).astype(bf16)
    ids = jnp.pad(ids.transpose(1, 0, 2), ((0, 0), (0, ID_ROWS - batches), (0, 0)))
    return place.reshape(-1), ids


def table_index(owner, row, rows, core):
    x, y, c = owner >> 3, (owner >> 1) & 3, owner & 1
    chip = jnp.where(c == 0, y * 4 + x, x * 4 + y)
    return (((c ^ core) * 16 + chip) * rows + row).reshape(-1)


def local(
    owner_shard, local_row, click_label, row_table, squared_sums, w_input, w_hidden, w_output
):
    rows, width = row_table.shape
    owner = owner_shard[..., 0]
    core = lax.axis_index("shard") & 1
    table_low, core = lax.optimization_barrier((row_table.astype(bf16), core))
    line = spread(table_low, "shard", FIRST).reshape(4 * rows, width)
    own = spread(line, "shard", SECOND).reshape(16 * rows, width)
    own, owner, local_row, click_label, core = lax.optimization_barrier(
        (own, owner, local_row, click_label, core)
    )
    other = lax.ppermute(own, "shard", SWAP)
    index = table_index(owner, local_row, rows, core)
    order = owner_order(core)
    place, ids = plan_slots(group_of(owner, core), local_row, own)
    labels = click_label.astype(f32)
    kept, sent, logits = run_main(
        index,
        place,
        order,
        own,
        other,
        labels,
        w_input,
        w_hidden,
        w_output.reshape(1, -1),
        ids,
    )
    got = lax.ppermute(sent, "shard", SWAP)
    dense = run_owner(got_kernel, rows, run_owner(kept_kernel, rows, kept), got)
    dense = dense.reshape(4, 4 * (rows + TERM_ROWS), width)
    line = exchange(dense, "shard", FIRST).astype(f32)
    line = jnp.sum(line, axis=0).astype(bf16).reshape(4, rows + TERM_ROWS, width)
    near = exchange(run_near(exchange(line, "shard", SECOND), rows), "grp", NEAR).astype(f32)
    grads = jnp.sum(near[:, 0:128], axis=0).astype(bf16)
    term = jnp.sum(near[:, 128:160], axis=0)
    term = term.reshape(8, 4, width).transpose(1, 0, 2).astype(bf16)
    far = jnp.concatenate([jnp.broadcast_to(grads[None], (4, 128, width)), term], axis=1)
    far = exchange(far, "grp", FAR)
    total = exchange(run_far(far), "grp", NEAR).reshape(rows, width)
    new_table, input_grad = run_final(total, row_table, squared_sums, far)
    return (new_table, logits, input_grad.reshape(-1))


def solution(mesh):
    in_specs = (
        P(None, ("grp", "shard"), None, None),
        P(None, ("grp", "shard"), None),
        P(None, ("grp", "shard")),
        P("shard", None),
        P("shard", None),
        P(),
        P(),
        P(),
    )
    out_specs = (P("shard", None), P(None, ("grp", "shard")), P(("grp", "shard")))
    return jax.shard_map(local, mesh=mesh, in_specs=in_specs, out_specs=out_specs, check_vma=False)
```

```python
import jax
import jax.numpy as jnp
from jax import lax
from jax.experimental import pallas as pl
from jax.experimental.pallas import tpu as pltpu
from jax.sharding import PartitionSpec as P

bf16 = jnp.bfloat16
f32 = jnp.float32
learn_rate = 0.1

SLOTS = 4
HOT = 4
LOOK = 16
SHARDS = 32
CAP = 128
BATCHES = 2
GRAD_ROWS = BATCHES * CAP
TERM_ROWS = 128
ID_ROWS = 16
SENT_ROWS = GRAD_ROWS + TERM_ROWS + ID_ROWS

FIRST = [[x * 8 + y * 2 for x in range(4)] for y in range(4)] + [
    [x * 8 + y * 2 + 1 for y in range(4)] for x in range(4)
]
SECOND = [[x * 8 + y * 2 for y in range(4)] for x in range(4)] + [
    [x * 8 + y * 2 + 1 for x in range(4)] for y in range(4)
]
SWAP = [(i, i ^ 1) for i in range(SHARDS)]
NEAR = [[4 * i + j for j in range(4)] for i in range(4)]
FAR = [[4 * i + j for i in range(4)] for j in range(4)]


def exchange(value, axis, groups=None):
    return lax.all_to_all(
        value, axis, split_axis=0, concat_axis=0, tiled=True, axis_index_groups=groups
    )


def spread(value, axis, groups):
    return exchange(jnp.broadcast_to(value[None], (4,) + value.shape), axis, groups)


def dot(a, b, dims):
    return lax.dot_general(a, b, (dims, ((), ())), preferred_element_type=f32)


def column(row):
    return jnp.transpose(jnp.broadcast_to(row, (128, 128)))[:, 0:1]


def main_kernel(
    index_ref,
    place_ref,
    order_ref,
    own_ref,
    other_ref,
    label_ref,
    w_input_ref,
    w_hidden_ref,
    w_output_ref,
    ids_ref,
    kept_ref,
    sent_ref,
    logit_ref,
    table_ref,
    pooled_ref,
    slot_ref,
    turn_ref,
    turned_ref,
    back_ref,
    term_ref,
):
    half = own_ref.shape[0]
    samples = pooled_ref.shape[0] // SLOTS

    def widen(step, carry):
        at = pl.multiple_of(step * 256, 256)
        table_ref[pl.ds(at, 256), :] = own_ref[pl.ds(at, 256), :].astype(f32)
        table_ref[pl.ds(half + at, 256), :] = other_ref[pl.ds(at, 256), :].astype(f32)
        return carry

    lax.fori_loop(0, half // 256, widen, 0)

    def look(step, carry):
        slot_ref[pl.ds(pl.multiple_of(step * 512, 512), 512), :] = jnp.zeros((512, 128), f32)
        for turn in range(16):
            sample = step * 16 + turn
            for slot in range(SLOTS):
                first = sample * LOOK + slot * HOT
                total = table_ref[pl.ds(index_ref[first], 1), :]
                for hot in range(1, HOT):
                    total = total + table_ref[pl.ds(index_ref[first + hot], 1), :]
                pooled_ref[pl.ds(slot * samples + sample, 1), :] = total
        return carry

    lax.fori_loop(0, samples // 16, look, 0)

    features = SLOTS * 128
    for slot in range(SLOTS):
        for b in range(BATCHES):
            block = pooled_ref[slot * samples + b * 128 : slot * samples + (b + 1) * 128, :]
            turn_ref[b * features + slot * 128 : b * features + (slot + 1) * 128, :] = jnp.transpose(block)
    turned_ref[...] = jnp.concatenate(
        [
            jnp.concatenate(
                [turn_ref[pl.ds(b * features + s, 16, stride=SHARDS), :] for s in range(SHARDS)],
                axis=0,
            ).astype(bf16)
            for b in range(BATCHES)
        ],
        axis=1,
    )
    pooled = jnp.concatenate(
        [pooled_ref[slot * samples : (slot + 1) * samples, :].astype(bf16) for slot in range(SLOTS)],
        axis=1,
    )
    w_input = w_input_ref[...]
    w_hidden = w_hidden_ref[...]
    w_output = w_output_ref[...].astype(f32)
    labels = jnp.concatenate([column(label_ref[b : b + 1, :]) for b in range(BATCHES)], axis=0)
    pre_one = dot(pooled, w_input, ((1,), (0,)))
    act_one = jnp.maximum(pre_one, 0.0).astype(bf16)
    pre_two = dot(act_one, w_hidden, ((1,), (0,)))
    act_two = jnp.maximum(pre_two, 0.0).astype(bf16).astype(f32)
    logits = jnp.sum(act_two * w_output, axis=1, keepdims=True)
    for b in range(BATCHES):
        part = jnp.broadcast_to(logits[b * 128 : (b + 1) * 128], (128, 128))
        logit_ref[b : b + 1, :] = jnp.transpose(part)[0:1, :]
    slope = jax.nn.sigmoid(logits) - labels
    back_two = jnp.where(pre_two > 0, slope * w_output, 0.0).astype(bf16)
    back_one = dot(back_two, w_hidden, ((1,), (1,)))
    back_one = jnp.where(pre_one > 0, back_one, 0.0).astype(bf16)
    back_in = dot(back_one, w_input, ((1,), (1,))).astype(bf16).astype(f32)
    for slot in range(SLOTS):
        pooled_ref[slot * samples : (slot + 1) * samples, :] = back_in[:, slot * 128 : (slot + 1) * 128]
    for j in range(8):
        back_ref[j] = back_one[:, j * 128 : (j + 1) * 128]

    def scatter(step, carry):
        term_ref[step] = dot(turned_ref[...], back_ref[step], ((1,), (0,)))
        for turn in range(32):
            sample = step * 32 + turn
            for slot in range(SLOTS):
                first = sample * LOOK + slot * HOT
                row = pooled_ref[pl.ds(slot * samples + sample, 1), :]
                for hot in range(HOT):
                    slot_ref[pl.ds(place_ref[first + hot], 1), :] = row
        return carry

    lax.fori_loop(0, samples // 32, scatter, 0)

    for target, base in ((sent_ref, SHARDS // 2), (kept_ref, 0)):

        def pack(owner, carry):
            at = pl.multiple_of((base + owner) * GRAD_ROWS, GRAD_ROWS)
            target[owner, 0:GRAD_ROWS, :] = slot_ref[pl.ds(at, GRAD_ROWS), :].astype(bf16)
            piece = pl.ds(pl.multiple_of(order_ref[base + owner] * 16, 16), 16)
            for j in range(8):
                target[owner, GRAD_ROWS + j * 16 : GRAD_ROWS + (j + 1) * 16, :] = term_ref[
                    j, piece, :
                ].astype(bf16)
            target[owner, GRAD_ROWS + TERM_ROWS : SENT_ROWS, :] = ids_ref[base + owner]
            return carry

        lax.fori_loop(0, SHARDS // 2, pack, 0, unroll=4)


def run_main(index, place, order, own, other, labels, w_input, w_hidden, w_output, ids):
    width = own.shape[1]
    samples = index.shape[0] // LOOK
    smem = pl.BlockSpec(memory_space=pltpu.SMEM)
    vmem = pl.BlockSpec(memory_space=pltpu.VMEM)
    return pl.pallas_call(
        main_kernel,
        out_shape=(
            jax.ShapeDtypeStruct((SHARDS // 2, SENT_ROWS, width), bf16),
            jax.ShapeDtypeStruct((SHARDS // 2, SENT_ROWS, width), bf16),
            jax.ShapeDtypeStruct((BATCHES, samples // BATCHES), f32),
        ),
        in_specs=[smem] * 3 + [vmem] * 7,
        out_specs=(vmem, vmem, vmem),
        scratch_shapes=[
            pltpu.VMEM((2 * own.shape[0], width), f32),
            pltpu.VMEM((samples * SLOTS, width), f32),
            pltpu.VMEM((SHARDS * GRAD_ROWS, width), f32),
            pltpu.VMEM((BATCHES * SLOTS * width, samples // BATCHES), f32),
            pltpu.VMEM((SLOTS * width, samples), bf16),
            pltpu.VMEM((8, samples, width), bf16),
            pltpu.VMEM((8, SLOTS * width, width), f32),
        ],
        compiler_params=pltpu.CompilerParams(vmem_limit_bytes=24 * 1024 * 1024),
        cost_estimate=pl.CostEstimate(
            flops=2_000_000_000, bytes_accessed=12_000_000, transcendentals=256
        ),
    )(index, place, order, own, other, labels, w_input, w_hidden, w_output, ids)


def row_code(row):
    return jnp.where(row < 256, row + 1, 255 - row).astype(f32).astype(bf16)


def add_source(source, owner, total, term):
    rows = lax.broadcasted_iota(jnp.int32, (total.shape[0], CAP), 0)
    names = row_code(rows)
    coded = source[owner, GRAD_ROWS + TERM_ROWS : SENT_ROWS, :]
    one, zero = jnp.ones((), bf16), jnp.zeros((), bf16)
    pick = jnp.concatenate(
        [jnp.where(names == coded[b : b + 1], one, zero) for b in range(BATCHES)], axis=1
    )
    total = total + dot(pick, source[owner, 0:GRAD_ROWS, :], ((1,), (0,)))
    return total, term + source[owner, GRAD_ROWS : GRAD_ROWS + TERM_ROWS, :].astype(f32)


def kept_kernel(kept_ref, out_ref):
    rows = out_ref.shape[1] - TERM_ROWS
    width = out_ref.shape[2]

    def step(owner, carry):
        total = jnp.zeros((rows, width), f32)
        term = jnp.zeros((TERM_ROWS, width), f32)
        total, term = add_source(kept_ref, owner, total, term)
        out_ref[owner, 0:rows, :] = total.astype(bf16)
        out_ref[owner, rows : rows + TERM_ROWS, :] = term.astype(bf16)
        return carry

    lax.fori_loop(0, out_ref.shape[0], step, 0, unroll=8)


def got_kernel(base_ref, got_ref, out_ref):
    rows = out_ref.shape[1] - TERM_ROWS

    def step(owner, carry):
        total = base_ref[owner, 0:rows, :].astype(f32)
        term = base_ref[owner, rows : rows + TERM_ROWS, :].astype(f32)
        total, term = add_source(got_ref, owner, total, term)
        out_ref[owner, 0:rows, :] = total.astype(bf16)
        out_ref[owner, rows : rows + TERM_ROWS, :] = term.astype(bf16)
        return carry

    lax.fori_loop(0, out_ref.shape[0], step, 0, unroll=8)


def run_owner(kernel, rows, *operands):
    owners, _, width = operands[0].shape
    vmem = pl.BlockSpec(memory_space=pltpu.VMEM)
    return pl.pallas_call(
        kernel,
        out_shape=jax.ShapeDtypeStruct((owners, rows + TERM_ROWS, width), bf16),
        in_specs=[vmem] * len(operands),
        out_specs=vmem,
        compiler_params=pltpu.CompilerParams(vmem_limit_bytes=32 * 1024 * 1024),
        cost_estimate=pl.CostEstimate(
            flops=550_000_000, bytes_accessed=5_000_000, transcendentals=0
        ),
    )(*operands)


def near_kernel(got_ref, out_ref, term_ref):
    rows = got_ref.shape[1] - TERM_ROWS
    part = rows // 4
    for k in range(4):
        total = got_ref[0, k * part : (k + 1) * part, :].astype(f32)
        for source in range(1, 4):
            total = total + got_ref[source, k * part : (k + 1) * part, :].astype(f32)
        out_ref[k, 0:part, :] = total.astype(bf16)
    term = got_ref[0, rows : rows + TERM_ROWS, :].astype(f32)
    for source in range(1, 4):
        term = term + got_ref[source, rows : rows + TERM_ROWS, :].astype(f32)
    term_ref[...] = term
    for k in range(4):
        out_ref[k, part : part + 32, :] = term_ref[pl.ds(k, 32, stride=4), :].astype(bf16)


def run_near(got, rows):
    width = got.shape[2]
    vmem = pl.BlockSpec(memory_space=pltpu.VMEM)
    return pl.pallas_call(
        near_kernel,
        out_shape=jax.ShapeDtypeStruct((4, rows // 4 + 32, width), bf16),
        in_specs=[vmem],
        out_specs=vmem,
        scratch_shapes=[pltpu.VMEM((TERM_ROWS, width), f32)],
        compiler_params=pltpu.CompilerParams(vmem_limit_bytes=32 * 1024 * 1024),
        cost_estimate=pl.CostEstimate(flops=500_000, bytes_accessed=900_000, transcendentals=0),
    )(got)


def sum_of(got_ref, first, last):
    total = got_ref[0, first:last].astype(f32)
    for source in range(1, 4):
        total = total + got_ref[source, first:last].astype(f32)
    return total


def far_kernel(got_ref, out_ref):
    total = sum_of(got_ref, 0, out_ref.shape[1]).astype(bf16)
    for k in range(4):
        out_ref[k] = total


def run_far(got):
    _, rows, width = got.shape
    vmem = pl.BlockSpec(memory_space=pltpu.VMEM)
    return pl.pallas_call(
        far_kernel,
        out_shape=jax.ShapeDtypeStruct((4, rows - 8, width), bf16),
        in_specs=[vmem],
        out_specs=vmem,
        compiler_params=pltpu.CompilerParams(vmem_limit_bytes=16 * 1024 * 1024),
        cost_estimate=pl.CostEstimate(flops=70_000, bytes_accessed=300_000, transcendentals=0),
    )(got)


def final_kernel(total_ref, table_ref, sums_ref, got_ref, new_ref, term_ref):
    grad = total_ref[...].astype(f32)
    new_sums = sums_ref[...] + grad * grad
    new_ref[...] = table_ref[...] - learn_rate * grad / jnp.sqrt(new_sums)
    term_ref[...] = sum_of(got_ref, got_ref.shape[1] - 8, got_ref.shape[1])


def run_final(total, table, sums, got):
    vmem = pl.BlockSpec(memory_space=pltpu.VMEM)
    return pl.pallas_call(
        final_kernel,
        out_shape=(
            jax.ShapeDtypeStruct(table.shape, f32),
            jax.ShapeDtypeStruct((8, table.shape[1]), f32),
        ),
        in_specs=[vmem] * 4,
        out_specs=(vmem, vmem),
        compiler_params=pltpu.CompilerParams(vmem_limit_bytes=16 * 1024 * 1024),
        cost_estimate=pl.CostEstimate(
            flops=500_000, bytes_accessed=1_000_000, transcendentals=65536
        ),
    )(total, table, sums, got)


def owner_order(core):
    group = jnp.arange(SHARDS, dtype=jnp.int32)
    c = (group >> 4) ^ core
    slow, fast = (group >> 2) & 3, group & 3
    x, y = jnp.where(c == 0, slow, fast), jnp.where(c == 0, fast, slow)
    return x * 8 + y * 2 + c


def group_of(owner, core):
    x, y, c = owner >> 3, (owner >> 1) & 3, owner & 1
    return (c ^ core) * 16 + jnp.where(c == 0, x * 4 + y, y * 4 + x)


def plan_slots(owner, row, after):
    batches, samples, looks = owner.shape
    names, steps, turn, batch, spots, after = lax.optimization_barrier(
        (
            jnp.arange(SHARDS, dtype=jnp.int32),
            jnp.arange(samples),
            jnp.arange(looks),
            jnp.arange(batches, dtype=jnp.int32),
            jnp.arange(CAP, dtype=jnp.int32),
            after,
        )
    )
    hit = (owner[..., None] == names).astype(bf16).reshape(batches, samples, looks * SHARDS)
    before = (steps[None, :] < steps[:, None]).astype(bf16)
    rank = jnp.einsum("ts,bsn->btn", before, hit, preferred_element_type=f32)
    counts = jnp.sum(hit.astype(f32), axis=1).reshape(batches, looks, SHARDS)
    base = jnp.sum(
        jnp.where((turn[None, :] < turn[:, None])[None, :, :, None], counts[:, None], 0.0), axis=2
    ).reshape(batches, 1, looks * SHARDS)
    spot = jnp.sum(
        (hit.astype(f32) * (rank + base)).reshape(batches, samples, looks, SHARDS), axis=3
    ).astype(jnp.int32)
    place = owner * GRAD_ROWS + batch[:, None, None] * CAP + spot
    flat_hit = hit.reshape(batches, samples * looks, SHARDS)
    coded = flat_hit * row_code(row).reshape(batches, -1, 1)
    where = (spot.reshape(batches, -1, 1) == spots).astype(bf16)
    ids = jnp.einsum("bin,bip->bnp", coded, where, preferred_element_type=f32).astype(bf16)
    ids = jnp.pad(ids.transpose(1, 0, 2), ((0, 0), (0, ID_ROWS - batches), (0, 0)))
    return place.reshape(-1), ids


def table_index(owner, row, rows, core):
    x, y, c = owner >> 3, (owner >> 1) & 3, owner & 1
    chip = jnp.where(c == 0, y * 4 + x, x * 4 + y)
    return (((c ^ core) * 16 + chip) * rows + row).reshape(-1)


def local(
    owner_shard, local_row, click_label, row_table, squared_sums, w_input, w_hidden, w_output
):
    rows, width = row_table.shape
    owner = owner_shard[..., 0]
    core = lax.axis_index("shard") & 1
    table_low, core = lax.optimization_barrier((row_table.astype(bf16), core))
    line = spread(table_low, "shard", FIRST).reshape(4 * rows, width)
    own = spread(line, "shard", SECOND).reshape(16 * rows, width)
    own, owner, local_row, click_label, core = lax.optimization_barrier(
        (own, owner, local_row, click_label, core)
    )
    other = lax.ppermute(own, "shard", SWAP)
    index = table_index(owner, local_row, rows, core)
    order = owner_order(core)
    place, ids = plan_slots(group_of(owner, core), local_row, own)
    labels = click_label.astype(f32)
    kept, sent, logits = run_main(
        index,
        place,
        order,
        own,
        other,
        labels,
        w_input,
        w_hidden,
        w_output.reshape(1, -1),
        ids,
    )
    got = lax.ppermute(sent, "shard", SWAP)
    dense = run_owner(got_kernel, rows, run_owner(kept_kernel, rows, kept), got)
    dense = dense.reshape(4, 4 * (rows + TERM_ROWS), width)
    line = exchange(dense, "shard", FIRST).astype(f32)
    line = jnp.sum(line, axis=0).astype(bf16).reshape(4, rows + TERM_ROWS, width)
    near = exchange(run_near(exchange(line, "shard", SECOND), rows), "grp", NEAR).astype(f32)
    grads = jnp.sum(near[:, 0:128], axis=0).astype(bf16)
    term = jnp.sum(near[:, 128:160], axis=0)
    term = term.reshape(8, 4, width).transpose(1, 0, 2).astype(bf16)
    far = jnp.concatenate([jnp.broadcast_to(grads[None], (4, 128, width)), term], axis=1)
    far = exchange(far, "grp", FAR)
    total = exchange(run_far(far), "grp", NEAR).reshape(rows, width)
    new_table, input_grad = run_final(total, row_table, squared_sums, far)
    return (new_table, logits, input_grad.reshape(-1))


def solution(mesh):
    in_specs = (
        P(None, ("grp", "shard"), None, None),
        P(None, ("grp", "shard"), None),
        P(None, ("grp", "shard")),
        P("shard", None),
        P("shard", None),
        P(),
        P(),
        P(),
    )
    out_specs = (P("shard", None), P(None, ("grp", "shard")), P(("grp", "shard")))
    return jax.shard_map(local, mesh=mesh, in_specs=in_specs, out_specs=out_specs, check_vma=False)
```

```python
import jax
import jax.numpy as jnp
from jax import lax
from jax.experimental import pallas as pl
from jax.experimental.pallas import tpu as pltpu
from jax.sharding import PartitionSpec as P

bf16 = jnp.bfloat16
f32 = jnp.float32
learn_rate = 0.1

SLOTS = 4
HOT = 4
LOOK = 16
SHARDS = 32
CAP = 128
BATCHES = 2
GRAD_ROWS = BATCHES * CAP
TERM_ROWS = 128
ID_ROWS = 16
SENT_ROWS = GRAD_ROWS + TERM_ROWS + ID_ROWS

FIRST = [[x * 8 + y * 2 for x in range(4)] for y in range(4)] + [
    [x * 8 + y * 2 + 1 for y in range(4)] for x in range(4)
]
SECOND = [[x * 8 + y * 2 for y in range(4)] for x in range(4)] + [
    [x * 8 + y * 2 + 1 for x in range(4)] for y in range(4)
]
SWAP = [(i, i ^ 1) for i in range(SHARDS)]
NEAR = [[4 * i + j for j in range(4)] for i in range(4)]
FAR = [[4 * i + j for i in range(4)] for j in range(4)]


def exchange(value, axis, groups=None):
    return lax.all_to_all(
        value, axis, split_axis=0, concat_axis=0, tiled=True, axis_index_groups=groups
    )


def spread(value, axis, groups):
    return exchange(jnp.broadcast_to(value[None], (4,) + value.shape), axis, groups)


def dot(a, b, dims):
    return lax.dot_general(a, b, (dims, ((), ())), preferred_element_type=f32)


def column(row):
    return jnp.transpose(jnp.broadcast_to(row, (128, 128)))[:, 0:1]


def main_kernel(
    index_ref,
    place_ref,
    order_ref,
    own_ref,
    other_hbm,
    label_ref,
    w_input_ref,
    w_hidden_hbm,
    w_output_ref,
    ids_ref,
    kept_ref,
    sent_ref,
    logit_ref,
    other_ref,
    w_hidden_ref,
    table_ref,
    pooled_ref,
    slot_ref,
    turn_ref,
    turned_ref,
    back_ref,
    term_ref,
    other_sem,
    weight_sem,
):
    half = own_ref.shape[0]
    samples = pooled_ref.shape[0] // SLOTS
    swap = pltpu.make_async_copy(other_hbm, other_ref, other_sem)
    swap.start()
    fetch = pltpu.make_async_copy(w_hidden_hbm, w_hidden_ref, weight_sem)
    fetch.start()

    for source, base in ((own_ref, 0), (other_ref, half)):
        if base:
            swap.wait()

        def widen(step, carry):
            at = pl.multiple_of(step * 256, 256)
            table_ref[pl.ds(base + at, 256), :] = source[pl.ds(at, 256), :].astype(f32)
            return carry

        lax.fori_loop(0, half // 256, widen, 0, unroll=2)

    def look(step, carry):
        slot_ref[pl.ds(pl.multiple_of(step * 512, 512), 512), :] = jnp.zeros((512, 128), f32)
        for turn in range(16):
            sample = step * 16 + turn
            for slot in range(SLOTS):
                first = sample * LOOK + slot * HOT
                total = table_ref[pl.ds(index_ref[first], 1), :]
                for hot in range(1, HOT):
                    total = total + table_ref[pl.ds(index_ref[first + hot], 1), :]
                pooled_ref[pl.ds(slot * samples + sample, 1), :] = total
        return carry

    lax.fori_loop(0, samples // 16, look, 0)

    features = SLOTS * 128
    for slot in range(SLOTS):
        for b in range(BATCHES):
            block = pooled_ref[slot * samples + b * 128 : slot * samples + (b + 1) * 128, :]
            turn_ref[b * features + slot * 128 : b * features + (slot + 1) * 128, :] = jnp.transpose(block)
    turned_ref[...] = jnp.concatenate(
        [
            jnp.concatenate(
                [turn_ref[pl.ds(b * features + s, 16, stride=SHARDS), :] for s in range(SHARDS)],
                axis=0,
            ).astype(bf16)
            for b in range(BATCHES)
        ],
        axis=1,
    )
    pooled = jnp.concatenate(
        [pooled_ref[slot * samples : (slot + 1) * samples, :].astype(bf16) for slot in range(SLOTS)],
        axis=1,
    )
    fetch.wait()
    w_input = w_input_ref[...]
    w_hidden = w_hidden_ref[...]
    w_output = w_output_ref[...].astype(f32)
    labels = jnp.concatenate([column(label_ref[b : b + 1, :]) for b in range(BATCHES)], axis=0)
    pre_one = dot(pooled, w_input, ((1,), (0,)))
    act_one = jnp.maximum(pre_one, 0.0).astype(bf16)
    pre_two = dot(act_one, w_hidden, ((1,), (0,)))
    act_two = jnp.maximum(pre_two, 0.0).astype(bf16).astype(f32)
    logits = jnp.sum(act_two * w_output, axis=1, keepdims=True)
    for b in range(BATCHES):
        part = jnp.broadcast_to(logits[b * 128 : (b + 1) * 128], (128, 128))
        logit_ref[b : b + 1, :] = jnp.transpose(part)[0:1, :]
    slope = jax.nn.sigmoid(logits) - labels
    back_two = jnp.where(pre_two > 0, slope * w_output, 0.0).astype(bf16)
    back_one = dot(back_two, w_hidden, ((1,), (1,)))
    back_one = jnp.where(pre_one > 0, back_one, 0.0).astype(bf16)
    back_in = dot(back_one, w_input, ((1,), (1,))).astype(bf16).astype(f32)
    for slot in range(SLOTS):
        pooled_ref[slot * samples : (slot + 1) * samples, :] = back_in[:, slot * 128 : (slot + 1) * 128]
    for j in range(8):
        back_ref[j] = back_one[:, j * 128 : (j + 1) * 128]

    def scatter(step, carry):
        term_ref[step] = dot(turned_ref[...], back_ref[step], ((1,), (0,)))
        for turn in range(32):
            sample = step * 32 + turn
            for slot in range(SLOTS):
                first = sample * LOOK + slot * HOT
                row = pooled_ref[pl.ds(slot * samples + sample, 1), :]
                for hot in range(HOT):
                    slot_ref[pl.ds(place_ref[first + hot], 1), :] = row
        return carry

    lax.fori_loop(0, samples // 32, scatter, 0)

    for target, base in ((sent_ref, SHARDS // 2), (kept_ref, 0)):

        def pack(owner, carry):
            at = pl.multiple_of((base + owner) * GRAD_ROWS, GRAD_ROWS)
            target[owner, 0:GRAD_ROWS, :] = slot_ref[pl.ds(at, GRAD_ROWS), :].astype(bf16)
            piece = pl.ds(pl.multiple_of(order_ref[base + owner] * 16, 16), 16)
            for j in range(8):
                target[owner, GRAD_ROWS + j * 16 : GRAD_ROWS + (j + 1) * 16, :] = term_ref[
                    j, piece, :
                ].astype(bf16)
            target[owner, GRAD_ROWS + TERM_ROWS : SENT_ROWS, :] = ids_ref[base + owner]
            return carry

        lax.fori_loop(0, SHARDS // 2, pack, 0, unroll=4)


def run_main(index, place, order, own, other, labels, w_input, w_hidden, w_output, ids):
    width = own.shape[1]
    samples = index.shape[0] // LOOK
    smem = pl.BlockSpec(memory_space=pltpu.SMEM)
    vmem = pl.BlockSpec(memory_space=pltpu.VMEM)
    anywhere = pl.BlockSpec(memory_space=pl.ANY)
    return pl.pallas_call(
        main_kernel,
        out_shape=(
            jax.ShapeDtypeStruct((SHARDS // 2, SENT_ROWS, width), bf16),
            jax.ShapeDtypeStruct((SHARDS // 2, SENT_ROWS, width), bf16),
            jax.ShapeDtypeStruct((BATCHES, samples // BATCHES), f32),
        ),
        in_specs=[smem] * 3 + [vmem, anywhere, vmem, vmem, anywhere, vmem, vmem],
        out_specs=(vmem, vmem, vmem),
        scratch_shapes=[
            pltpu.VMEM(other.shape, bf16),
            pltpu.VMEM(w_hidden.shape, bf16),
            pltpu.VMEM((2 * own.shape[0], width), f32),
            pltpu.VMEM((samples * SLOTS, width), f32),
            pltpu.VMEM((SHARDS * GRAD_ROWS, width), f32),
            pltpu.VMEM((BATCHES * SLOTS * width, samples // BATCHES), f32),
            pltpu.VMEM((SLOTS * width, samples), bf16),
            pltpu.VMEM((8, samples, width), bf16),
            pltpu.VMEM((8, SLOTS * width, width), f32),
            pltpu.SemaphoreType.DMA(()),
            pltpu.SemaphoreType.DMA(()),
        ],
        compiler_params=pltpu.CompilerParams(vmem_limit_bytes=44 * 1024 * 1024),
        cost_estimate=pl.CostEstimate(
            flops=2_000_000_000, bytes_accessed=12_000_000, transcendentals=256
        ),
    )(index, place, order, own, other, labels, w_input, w_hidden, w_output, ids)


def row_code(row):
    return jnp.where(row < 256, row + 1, 255 - row).astype(f32).astype(bf16)


def add_source(source, owner, total, term):
    rows = lax.broadcasted_iota(jnp.int32, (total.shape[0], CAP), 0)
    names = row_code(rows)
    coded = source[owner, GRAD_ROWS + TERM_ROWS : SENT_ROWS, :]
    one, zero = jnp.ones((), bf16), jnp.zeros((), bf16)
    pick = jnp.concatenate(
        [jnp.where(names == coded[b : b + 1], one, zero) for b in range(BATCHES)], axis=1
    )
    total = total + dot(pick, source[owner, 0:GRAD_ROWS, :], ((1,), (0,)))
    return total, term + source[owner, GRAD_ROWS : GRAD_ROWS + TERM_ROWS, :].astype(f32)


def kept_kernel(kept_ref, out_ref):
    rows = out_ref.shape[1] - TERM_ROWS
    width = out_ref.shape[2]

    def step(owner, carry):
        total = jnp.zeros((rows, width), f32)
        term = jnp.zeros((TERM_ROWS, width), f32)
        total, term = add_source(kept_ref, owner, total, term)
        out_ref[owner, 0:rows, :] = total.astype(bf16)
        out_ref[owner, rows : rows + TERM_ROWS, :] = term.astype(bf16)
        return carry

    lax.fori_loop(0, out_ref.shape[0], step, 0, unroll=8)


def got_kernel(base_ref, got_ref, out_ref):
    rows = out_ref.shape[1] - TERM_ROWS

    def step(owner, carry):
        total = base_ref[owner, 0:rows, :].astype(f32)
        term = base_ref[owner, rows : rows + TERM_ROWS, :].astype(f32)
        total, term = add_source(got_ref, owner, total, term)
        out_ref[owner, 0:rows, :] = total.astype(bf16)
        out_ref[owner, rows : rows + TERM_ROWS, :] = term.astype(bf16)
        return carry

    lax.fori_loop(0, out_ref.shape[0], step, 0, unroll=8)


def run_owner(kernel, rows, *operands):
    owners, _, width = operands[0].shape
    vmem = pl.BlockSpec(memory_space=pltpu.VMEM)
    return pl.pallas_call(
        kernel,
        out_shape=jax.ShapeDtypeStruct((owners, rows + TERM_ROWS, width), bf16),
        in_specs=[vmem] * len(operands),
        out_specs=vmem,
        compiler_params=pltpu.CompilerParams(vmem_limit_bytes=32 * 1024 * 1024),
        cost_estimate=pl.CostEstimate(
            flops=550_000_000, bytes_accessed=5_000_000, transcendentals=0
        ),
    )(*operands)


def near_kernel(got_ref, out_ref, term_ref):
    rows = got_ref.shape[1] - TERM_ROWS
    part = rows // 4
    for k in range(4):
        total = got_ref[0, k * part : (k + 1) * part, :].astype(f32)
        for source in range(1, 4):
            total = total + got_ref[source, k * part : (k + 1) * part, :].astype(f32)
        out_ref[k, 0:part, :] = total.astype(bf16)
    term = got_ref[0, rows : rows + TERM_ROWS, :].astype(f32)
    for source in range(1, 4):
        term = term + got_ref[source, rows : rows + TERM_ROWS, :].astype(f32)
    term_ref[...] = term
    for k in range(4):
        out_ref[k, part : part + 32, :] = term_ref[pl.ds(k, 32, stride=4), :].astype(bf16)


def run_near(got, rows):
    width = got.shape[2]
    vmem = pl.BlockSpec(memory_space=pltpu.VMEM)
    return pl.pallas_call(
        near_kernel,
        out_shape=jax.ShapeDtypeStruct((4, rows // 4 + 32, width), bf16),
        in_specs=[vmem],
        out_specs=vmem,
        scratch_shapes=[pltpu.VMEM((TERM_ROWS, width), f32)],
        compiler_params=pltpu.CompilerParams(vmem_limit_bytes=32 * 1024 * 1024),
        cost_estimate=pl.CostEstimate(flops=500_000, bytes_accessed=900_000, transcendentals=0),
    )(got)


def sum_of(got_ref, first, last):
    total = got_ref[0, first:last].astype(f32)
    for source in range(1, 4):
        total = total + got_ref[source, first:last].astype(f32)
    return total


def far_kernel(got_ref, out_ref):
    total = sum_of(got_ref, 0, out_ref.shape[1]).astype(bf16)
    for k in range(4):
        out_ref[k] = total


def run_far(got):
    _, rows, width = got.shape
    vmem = pl.BlockSpec(memory_space=pltpu.VMEM)
    return pl.pallas_call(
        far_kernel,
        out_shape=jax.ShapeDtypeStruct((4, rows - 8, width), bf16),
        in_specs=[vmem],
        out_specs=vmem,
        compiler_params=pltpu.CompilerParams(vmem_limit_bytes=16 * 1024 * 1024),
        cost_estimate=pl.CostEstimate(flops=70_000, bytes_accessed=300_000, transcendentals=0),
    )(got)


def final_kernel(total_ref, table_ref, sums_ref, got_ref, new_ref, term_ref):
    grad = total_ref[...].astype(f32)
    new_sums = sums_ref[...] + grad * grad
    new_ref[...] = table_ref[...] - learn_rate * grad / jnp.sqrt(new_sums)
    term_ref[...] = sum_of(got_ref, got_ref.shape[1] - 8, got_ref.shape[1])


def run_final(total, table, sums, got):
    vmem = pl.BlockSpec(memory_space=pltpu.VMEM)
    return pl.pallas_call(
        final_kernel,
        out_shape=(
            jax.ShapeDtypeStruct(table.shape, f32),
            jax.ShapeDtypeStruct((8, table.shape[1]), f32),
        ),
        in_specs=[vmem] * 4,
        out_specs=(vmem, vmem),
        compiler_params=pltpu.CompilerParams(vmem_limit_bytes=16 * 1024 * 1024),
        cost_estimate=pl.CostEstimate(
            flops=500_000, bytes_accessed=1_000_000, transcendentals=65536
        ),
    )(total, table, sums, got)


def owner_order(core):
    group = jnp.arange(SHARDS, dtype=jnp.int32)
    c = (group >> 4) ^ core
    slow, fast = (group >> 2) & 3, group & 3
    x, y = jnp.where(c == 0, slow, fast), jnp.where(c == 0, fast, slow)
    return x * 8 + y * 2 + c


def group_of(owner, core):
    x, y, c = owner >> 3, (owner >> 1) & 3, owner & 1
    return (c ^ core) * 16 + jnp.where(c == 0, x * 4 + y, y * 4 + x)


def plan_slots(owner, row, after):
    batches, samples, looks = owner.shape
    names, steps, turn, batch, spots, after = lax.optimization_barrier(
        (
            jnp.arange(SHARDS, dtype=jnp.int32),
            jnp.arange(samples),
            jnp.arange(looks),
            jnp.arange(batches, dtype=jnp.int32),
            jnp.arange(CAP, dtype=jnp.int32),
            after,
        )
    )
    hit = (owner[..., None] == names).astype(bf16).reshape(batches, samples, looks * SHARDS)
    before = (steps[None, :] < steps[:, None]).astype(bf16)
    rank = jnp.einsum("ts,bsn->btn", before, hit, preferred_element_type=f32)
    counts = jnp.sum(hit.astype(f32), axis=1).reshape(batches, looks, SHARDS)
    base = jnp.sum(
        jnp.where((turn[None, :] < turn[:, None])[None, :, :, None], counts[:, None], 0.0), axis=2
    ).reshape(batches, 1, looks * SHARDS)
    spot = jnp.sum(
        (hit.astype(f32) * (rank + base)).reshape(batches, samples, looks, SHARDS), axis=3
    ).astype(jnp.int32)
    place = owner * GRAD_ROWS + batch[:, None, None] * CAP + spot
    flat_hit = hit.reshape(batches, samples * looks, SHARDS)
    coded = flat_hit * row_code(row).reshape(batches, -1, 1)
    where = (spot.reshape(batches, -1, 1) == spots).astype(bf16)
    ids = jnp.einsum("bin,bip->bnp", coded, where, preferred_element_type=f32).astype(bf16)
    ids = jnp.pad(ids.transpose(1, 0, 2), ((0, 0), (0, ID_ROWS - batches), (0, 0)))
    return place.reshape(-1), ids


def table_index(owner, row, rows, core):
    x, y, c = owner >> 3, (owner >> 1) & 3, owner & 1
    chip = jnp.where(c == 0, y * 4 + x, x * 4 + y)
    return (((c ^ core) * 16 + chip) * rows + row).reshape(-1)


def local(
    owner_shard, local_row, click_label, row_table, squared_sums, w_input, w_hidden, w_output
):
    rows, width = row_table.shape
    owner = owner_shard[..., 0]
    core = lax.axis_index("shard") & 1
    table_low, core = lax.optimization_barrier((row_table.astype(bf16), core))
    line = spread(table_low, "shard", FIRST).reshape(4 * rows, width)
    own = spread(line, "shard", SECOND).reshape(16 * rows, width)
    own, owner, local_row, click_label, core = lax.optimization_barrier(
        (own, owner, local_row, click_label, core)
    )
    other = lax.ppermute(own, "shard", SWAP)
    index = table_index(owner, local_row, rows, core)
    order = owner_order(core)
    place, ids = plan_slots(group_of(owner, core), local_row, own)
    labels = click_label.astype(f32)
    kept, sent, logits = run_main(
        index,
        place,
        order,
        own,
        other,
        labels,
        w_input,
        w_hidden,
        w_output.reshape(1, -1),
        ids,
    )
    got = lax.ppermute(sent, "shard", SWAP)
    dense = run_owner(got_kernel, rows, run_owner(kept_kernel, rows, kept), got)
    dense = dense.reshape(4, 4 * (rows + TERM_ROWS), width)
    line = exchange(dense, "shard", FIRST).astype(f32)
    line = jnp.sum(line, axis=0).astype(bf16).reshape(4, rows + TERM_ROWS, width)
    near = exchange(run_near(exchange(line, "shard", SECOND), rows), "grp", NEAR).astype(f32)
    grads = jnp.sum(near[:, 0:128], axis=0).astype(bf16)
    term = jnp.sum(near[:, 128:160], axis=0)
    term = term.reshape(8, 4, width).transpose(1, 0, 2).astype(bf16)
    far = jnp.concatenate([jnp.broadcast_to(grads[None], (4, 128, width)), term], axis=1)
    far = exchange(far, "grp", FAR)
    total = exchange(run_far(far), "grp", NEAR).reshape(rows, width)
    new_table, input_grad = run_final(total, row_table, squared_sums, far)
    return (new_table, logits, input_grad.reshape(-1))


def solution(mesh):
    in_specs = (
        P(None, ("grp", "shard"), None, None),
        P(None, ("grp", "shard"), None),
        P(None, ("grp", "shard")),
        P("shard", None),
        P("shard", None),
        P(),
        P(),
        P(),
    )
    out_specs = (P("shard", None), P(None, ("grp", "shard")), P(("grp", "shard")))
    return jax.shard_map(local, mesh=mesh, in_specs=in_specs, out_specs=out_specs, check_vma=False)
```

```python
import jax
import jax.numpy as jnp
from jax import lax
from jax.experimental import pallas as pl
from jax.experimental.pallas import tpu as pltpu
from jax.sharding import PartitionSpec as P

bf16 = jnp.bfloat16
f32 = jnp.float32
learn_rate = 0.1

SLOTS = 4
HOT = 4
LOOK = 16
SHARDS = 32
CAP = 128
BATCHES = 2
GRAD_ROWS = BATCHES * CAP
TERM_ROWS = 128
ID_ROWS = 16
SENT_ROWS = GRAD_ROWS + TERM_ROWS + ID_ROWS

FIRST = [[x * 8 + y * 2 for x in range(4)] for y in range(4)] + [
    [x * 8 + y * 2 + 1 for y in range(4)] for x in range(4)
]
SECOND = [[x * 8 + y * 2 for y in range(4)] for x in range(4)] + [
    [x * 8 + y * 2 + 1 for x in range(4)] for y in range(4)
]
SWAP = [(i, i ^ 1) for i in range(SHARDS)]
NEAR = [[4 * i + j for j in range(4)] for i in range(4)]
FAR = [[4 * i + j for i in range(4)] for j in range(4)]


def exchange(value, axis, groups=None):
    return lax.all_to_all(
        value, axis, split_axis=0, concat_axis=0, tiled=True, axis_index_groups=groups
    )


def spread(value, axis, groups):
    return exchange(jnp.broadcast_to(value[None], (4,) + value.shape), axis, groups)


def dot(a, b, dims):
    return lax.dot_general(a, b, (dims, ((), ())), preferred_element_type=f32)


def column(row):
    return jnp.transpose(jnp.broadcast_to(row, (128, 128)))[:, 0:1]


def main_kernel(
    index_ref,
    place_ref,
    order_ref,
    own_ref,
    other_ref,
    label_ref,
    w_input_ref,
    w_hidden_hbm,
    w_output_ref,
    ids_ref,
    kept_ref,
    sent_ref,
    logit_ref,
    w_hidden_ref,
    table_ref,
    pooled_ref,
    slot_ref,
    turn_ref,
    turned_ref,
    back_ref,
    term_ref,
    weight_sem,
):
    half = own_ref.shape[0]
    samples = pooled_ref.shape[0] // SLOTS
    fetch = pltpu.make_async_copy(w_hidden_hbm, w_hidden_ref, weight_sem)
    fetch.start()

    def widen(step, carry):
        at = pl.multiple_of(step * 256, 256)
        table_ref[pl.ds(at, 256), :] = own_ref[pl.ds(at, 256), :].astype(f32)
        table_ref[pl.ds(half + at, 256), :] = other_ref[pl.ds(at, 256), :].astype(f32)
        return carry

    lax.fori_loop(0, half // 256, widen, 0)

    def look(step, carry):
        slot_ref[pl.ds(pl.multiple_of(step * 512, 512), 512), :] = jnp.zeros((512, 128), f32)
        for turn in range(16):
            sample = step * 16 + turn
            for slot in range(SLOTS):
                first = sample * LOOK + slot * HOT
                total = table_ref[pl.ds(index_ref[first], 1), :]
                for hot in range(1, HOT):
                    total = total + table_ref[pl.ds(index_ref[first + hot], 1), :]
                pooled_ref[pl.ds(slot * samples + sample, 1), :] = total
        return carry

    lax.fori_loop(0, samples // 16, look, 0)

    features = SLOTS * 128
    for slot in range(SLOTS):
        for b in range(BATCHES):
            block = pooled_ref[slot * samples + b * 128 : slot * samples + (b + 1) * 128, :]
            turn_ref[b * features + slot * 128 : b * features + (slot + 1) * 128, :] = jnp.transpose(block)
    turned_ref[...] = jnp.concatenate(
        [
            jnp.concatenate(
                [turn_ref[pl.ds(b * features + s, 16, stride=SHARDS), :] for s in range(SHARDS)],
                axis=0,
            ).astype(bf16)
            for b in range(BATCHES)
        ],
        axis=1,
    )
    pooled = jnp.concatenate(
        [pooled_ref[slot * samples : (slot + 1) * samples, :].astype(bf16) for slot in range(SLOTS)],
        axis=1,
    )
    fetch.wait()
    w_input = w_input_ref[...]
    w_hidden = w_hidden_ref[...]
    w_output = w_output_ref[...].astype(f32)
    labels = jnp.concatenate([column(label_ref[b : b + 1, :]) for b in range(BATCHES)], axis=0)
    pre_one = dot(pooled, w_input, ((1,), (0,)))
    act_one = jnp.maximum(pre_one, 0.0).astype(bf16)
    pre_two = dot(act_one, w_hidden, ((1,), (0,)))
    act_two = jnp.maximum(pre_two, 0.0).astype(bf16).astype(f32)
    logits = jnp.sum(act_two * w_output, axis=1, keepdims=True)
    for b in range(BATCHES):
        part = jnp.broadcast_to(logits[b * 128 : (b + 1) * 128], (128, 128))
        logit_ref[b : b + 1, :] = jnp.transpose(part)[0:1, :]
    slope = jax.nn.sigmoid(logits) - labels
    back_two = jnp.where(pre_two > 0, slope * w_output, 0.0).astype(bf16)
    back_one = dot(back_two, w_hidden, ((1,), (1,)))
    back_one = jnp.where(pre_one > 0, back_one, 0.0).astype(bf16)
    back_in = dot(back_one, w_input, ((1,), (1,))).astype(bf16).astype(f32)
    for slot in range(SLOTS):
        pooled_ref[slot * samples : (slot + 1) * samples, :] = back_in[:, slot * 128 : (slot + 1) * 128]
    for j in range(8):
        back_ref[j] = back_one[:, j * 128 : (j + 1) * 128]

    def scatter(step, carry):
        term_ref[step] = dot(turned_ref[...], back_ref[step], ((1,), (0,)))
        for turn in range(32):
            sample = step * 32 + turn
            for slot in range(SLOTS):
                first = sample * LOOK + slot * HOT
                row = pooled_ref[pl.ds(slot * samples + sample, 1), :]
                for hot in range(HOT):
                    slot_ref[pl.ds(place_ref[first + hot], 1), :] = row
        return carry

    lax.fori_loop(0, samples // 32, scatter, 0)

    for target, base in ((sent_ref, SHARDS // 2), (kept_ref, 0)):

        def pack(owner, carry):
            at = pl.multiple_of((base + owner) * GRAD_ROWS, GRAD_ROWS)
            target[owner, 0:GRAD_ROWS, :] = slot_ref[pl.ds(at, GRAD_ROWS), :].astype(bf16)
            piece = pl.ds(pl.multiple_of(order_ref[base + owner] * 16, 16), 16)
            for j in range(8):
                target[owner, GRAD_ROWS + j * 16 : GRAD_ROWS + (j + 1) * 16, :] = term_ref[
                    j, piece, :
                ].astype(bf16)
            target[owner, GRAD_ROWS + TERM_ROWS : SENT_ROWS, :] = ids_ref[base + owner]
            return carry

        lax.fori_loop(0, SHARDS // 2, pack, 0, unroll=4)


def run_main(index, place, order, own, other, labels, w_input, w_hidden, w_output, ids):
    width = own.shape[1]
    samples = index.shape[0] // LOOK
    smem = pl.BlockSpec(memory_space=pltpu.SMEM)
    vmem = pl.BlockSpec(memory_space=pltpu.VMEM)
    return pl.pallas_call(
        main_kernel,
        out_shape=(
            jax.ShapeDtypeStruct((SHARDS // 2, SENT_ROWS, width), bf16),
            jax.ShapeDtypeStruct((SHARDS // 2, SENT_ROWS, width), bf16),
            jax.ShapeDtypeStruct((BATCHES, samples // BATCHES), f32),
        ),
        in_specs=[smem] * 3 + [vmem] * 4 + [pl.BlockSpec(memory_space=pl.ANY)] + [vmem] * 2,
        out_specs=(vmem, vmem, vmem),
        scratch_shapes=[
            pltpu.VMEM(w_hidden.shape, bf16),
            pltpu.VMEM((2 * own.shape[0], width), f32),
            pltpu.VMEM((samples * SLOTS, width), f32),
            pltpu.VMEM((SHARDS * GRAD_ROWS, width), f32),
            pltpu.VMEM((BATCHES * SLOTS * width, samples // BATCHES), f32),
            pltpu.VMEM((SLOTS * width, samples), bf16),
            pltpu.VMEM((8, samples, width), bf16),
            pltpu.VMEM((8, SLOTS * width, width), f32),
            pltpu.SemaphoreType.DMA(()),
        ],
        compiler_params=pltpu.CompilerParams(vmem_limit_bytes=44 * 1024 * 1024),
        cost_estimate=pl.CostEstimate(
            flops=2_000_000_000, bytes_accessed=12_000_000, transcendentals=256
        ),
    )(index, place, order, own, other, labels, w_input, w_hidden, w_output, ids)


def row_code(row):
    return jnp.where(row < 256, row + 1, 255 - row).astype(f32).astype(bf16)


def add_source(source, owner, total, term):
    rows = lax.broadcasted_iota(jnp.int32, (total.shape[0], CAP), 0)
    names = row_code(rows)
    coded = source[owner, GRAD_ROWS + TERM_ROWS : SENT_ROWS, :]
    one, zero = jnp.ones((), bf16), jnp.zeros((), bf16)
    pick = jnp.concatenate(
        [jnp.where(names == coded[b : b + 1], one, zero) for b in range(BATCHES)], axis=1
    )
    total = total + dot(pick, source[owner, 0:GRAD_ROWS, :], ((1,), (0,)))
    return total, term + source[owner, GRAD_ROWS : GRAD_ROWS + TERM_ROWS, :].astype(f32)


def kept_kernel(kept_ref, out_ref):
    rows = out_ref.shape[1] - TERM_ROWS
    width = out_ref.shape[2]

    def step(owner, carry):
        total = jnp.zeros((rows, width), f32)
        term = jnp.zeros((TERM_ROWS, width), f32)
        total, term = add_source(kept_ref, owner, total, term)
        out_ref[owner, 0:rows, :] = total.astype(bf16)
        out_ref[owner, rows : rows + TERM_ROWS, :] = term.astype(bf16)
        return carry

    lax.fori_loop(0, out_ref.shape[0], step, 0, unroll=8)


def got_kernel(base_ref, got_ref, out_ref):
    rows = out_ref.shape[1] - TERM_ROWS

    def step(owner, carry):
        total = base_ref[owner, 0:rows, :].astype(f32)
        term = base_ref[owner, rows : rows + TERM_ROWS, :].astype(f32)
        total, term = add_source(got_ref, owner, total, term)
        out_ref[owner, 0:rows, :] = total.astype(bf16)
        out_ref[owner, rows : rows + TERM_ROWS, :] = term.astype(bf16)
        return carry

    lax.fori_loop(0, out_ref.shape[0], step, 0, unroll=8)


def run_owner(kernel, rows, *operands):
    owners, _, width = operands[0].shape
    vmem = pl.BlockSpec(memory_space=pltpu.VMEM)
    return pl.pallas_call(
        kernel,
        out_shape=jax.ShapeDtypeStruct((owners, rows + TERM_ROWS, width), bf16),
        in_specs=[vmem] * len(operands),
        out_specs=vmem,
        compiler_params=pltpu.CompilerParams(vmem_limit_bytes=32 * 1024 * 1024),
        cost_estimate=pl.CostEstimate(
            flops=550_000_000, bytes_accessed=5_000_000, transcendentals=0
        ),
    )(*operands)


def near_kernel(got_ref, out_ref, term_ref):
    rows = got_ref.shape[1] - TERM_ROWS
    part = rows // 4
    for k in range(4):
        total = got_ref[0, k * part : (k + 1) * part, :].astype(f32)
        for source in range(1, 4):
            total = total + got_ref[source, k * part : (k + 1) * part, :].astype(f32)
        out_ref[k, 0:part, :] = total.astype(bf16)
    term = got_ref[0, rows : rows + TERM_ROWS, :].astype(f32)
    for source in range(1, 4):
        term = term + got_ref[source, rows : rows + TERM_ROWS, :].astype(f32)
    term_ref[...] = term
    for k in range(4):
        out_ref[k, part : part + 32, :] = term_ref[pl.ds(k, 32, stride=4), :].astype(bf16)


def run_near(got, rows):
    width = got.shape[2]
    vmem = pl.BlockSpec(memory_space=pltpu.VMEM)
    return pl.pallas_call(
        near_kernel,
        out_shape=jax.ShapeDtypeStruct((4, rows // 4 + 32, width), bf16),
        in_specs=[vmem],
        out_specs=vmem,
        scratch_shapes=[pltpu.VMEM((TERM_ROWS, width), f32)],
        compiler_params=pltpu.CompilerParams(vmem_limit_bytes=32 * 1024 * 1024),
        cost_estimate=pl.CostEstimate(flops=500_000, bytes_accessed=900_000, transcendentals=0),
    )(got)


def sum_of(got_ref, first, last):
    total = got_ref[0, first:last].astype(f32)
    for source in range(1, 4):
        total = total + got_ref[source, first:last].astype(f32)
    return total


def far_kernel(got_ref, out_ref):
    total = sum_of(got_ref, 0, out_ref.shape[1]).astype(bf16)
    for k in range(4):
        out_ref[k] = total


def run_far(got):
    _, rows, width = got.shape
    vmem = pl.BlockSpec(memory_space=pltpu.VMEM)
    return pl.pallas_call(
        far_kernel,
        out_shape=jax.ShapeDtypeStruct((4, rows - 8, width), bf16),
        in_specs=[vmem],
        out_specs=vmem,
        compiler_params=pltpu.CompilerParams(vmem_limit_bytes=16 * 1024 * 1024),
        cost_estimate=pl.CostEstimate(flops=70_000, bytes_accessed=300_000, transcendentals=0),
    )(got)


def final_kernel(total_ref, table_ref, sums_ref, got_ref, new_ref, term_ref):
    grad = total_ref[...].astype(f32)
    new_sums = sums_ref[...] + grad * grad
    new_ref[...] = table_ref[...] - learn_rate * grad / jnp.sqrt(new_sums)
    term_ref[...] = sum_of(got_ref, got_ref.shape[1] - 8, got_ref.shape[1])


def run_final(total, table, sums, got):
    vmem = pl.BlockSpec(memory_space=pltpu.VMEM)
    return pl.pallas_call(
        final_kernel,
        out_shape=(
            jax.ShapeDtypeStruct(table.shape, f32),
            jax.ShapeDtypeStruct((8, table.shape[1]), f32),
        ),
        in_specs=[vmem] * 4,
        out_specs=(vmem, vmem),
        compiler_params=pltpu.CompilerParams(vmem_limit_bytes=16 * 1024 * 1024),
        cost_estimate=pl.CostEstimate(
            flops=500_000, bytes_accessed=1_000_000, transcendentals=65536
        ),
    )(total, table, sums, got)


def owner_order(core):
    group = jnp.arange(SHARDS, dtype=jnp.int32)
    c = (group >> 4) ^ core
    slow, fast = (group >> 2) & 3, group & 3
    x, y = jnp.where(c == 0, slow, fast), jnp.where(c == 0, fast, slow)
    return x * 8 + y * 2 + c


def group_of(owner, core):
    x, y, c = owner >> 3, (owner >> 1) & 3, owner & 1
    return (c ^ core) * 16 + jnp.where(c == 0, x * 4 + y, y * 4 + x)


def plan_slots(owner, row, after):
    batches, samples, looks = owner.shape
    names, steps, turn, batch, spots, after = lax.optimization_barrier(
        (
            jnp.arange(SHARDS, dtype=jnp.int32),
            jnp.arange(samples),
            jnp.arange(looks),
            jnp.arange(batches, dtype=jnp.int32),
            jnp.arange(CAP, dtype=jnp.int32),
            after,
        )
    )
    hit = (owner[..., None] == names).astype(bf16).reshape(batches, samples, looks * SHARDS)
    before = (steps[None, :] < steps[:, None]).astype(bf16)
    rank = jnp.einsum("ts,bsn->btn", before, hit, preferred_element_type=f32)
    counts = jnp.sum(hit.astype(f32), axis=1).reshape(batches, looks, SHARDS)
    base = jnp.sum(
        jnp.where((turn[None, :] < turn[:, None])[None, :, :, None], counts[:, None], 0.0), axis=2
    ).reshape(batches, 1, looks * SHARDS)
    spot = jnp.sum(
        (hit.astype(f32) * (rank + base)).reshape(batches, samples, looks, SHARDS), axis=3
    ).astype(jnp.int32)
    place = owner * GRAD_ROWS + batch[:, None, None] * CAP + spot
    flat_hit = hit.reshape(batches, samples * looks, SHARDS)
    coded = flat_hit * row_code(row).reshape(batches, -1, 1)
    where = (spot.reshape(batches, -1, 1) == spots).astype(bf16)
    ids = jnp.einsum("bin,bip->bnp", coded, where, preferred_element_type=f32).astype(bf16)
    ids = jnp.pad(ids.transpose(1, 0, 2), ((0, 0), (0, ID_ROWS - batches), (0, 0)))
    return place.reshape(-1), ids


def table_index(owner, row, rows, core):
    x, y, c = owner >> 3, (owner >> 1) & 3, owner & 1
    chip = jnp.where(c == 0, y * 4 + x, x * 4 + y)
    return (((c ^ core) * 16 + chip) * rows + row).reshape(-1)


def local(
    owner_shard, local_row, click_label, row_table, squared_sums, w_input, w_hidden, w_output
):
    rows, width = row_table.shape
    owner = owner_shard[..., 0]
    core = lax.axis_index("shard") & 1
    table_low, core = lax.optimization_barrier((row_table.astype(bf16), core))
    line = spread(table_low, "shard", FIRST).reshape(4 * rows, width)
    own = spread(line, "shard", SECOND).reshape(16 * rows, width)
    own, owner, local_row, click_label, core = lax.optimization_barrier(
        (own, owner, local_row, click_label, core)
    )
    other = lax.ppermute(own, "shard", SWAP)
    index = table_index(owner, local_row, rows, core)
    order = owner_order(core)
    place, ids = plan_slots(group_of(owner, core), local_row, own)
    labels = click_label.astype(f32)
    kept, sent, logits = run_main(
        index,
        place,
        order,
        own,
        other,
        labels,
        w_input,
        w_hidden,
        w_output.reshape(1, -1),
        ids,
    )
    got = lax.ppermute(sent, "shard", SWAP)
    dense = run_owner(got_kernel, rows, run_owner(kept_kernel, rows, kept), got)
    dense = dense.reshape(4, 4 * (rows + TERM_ROWS), width)
    line = exchange(dense, "shard", FIRST).astype(f32)
    line = jnp.sum(line, axis=0).astype(bf16).reshape(4, rows + TERM_ROWS, width)
    near = exchange(run_near(exchange(line, "shard", SECOND), rows), "grp", NEAR).astype(f32)
    grads = jnp.sum(near[:, 0:128], axis=0).astype(bf16)
    term = jnp.sum(near[:, 128:160], axis=0)
    term = term.reshape(8, 4, width).transpose(1, 0, 2).astype(bf16)
    far = jnp.concatenate([jnp.broadcast_to(grads[None], (4, 128, width)), term], axis=1)
    far = exchange(far, "grp", FAR)
    total = exchange(run_far(far), "grp", NEAR).reshape(rows, width)
    new_table, input_grad = run_final(total, row_table, squared_sums, far)
    return (new_table, logits, input_grad.reshape(-1))


def solution(mesh):
    in_specs = (
        P(None, ("grp", "shard"), None, None),
        P(None, ("grp", "shard"), None),
        P(None, ("grp", "shard")),
        P("shard", None),
        P("shard", None),
        P(),
        P(),
        P(),
    )
    out_specs = (P("shard", None), P(None, ("grp", "shard")), P(("grp", "shard")))
    return jax.shard_map(local, mesh=mesh, in_specs=in_specs, out_specs=out_specs, check_vma=False)
```

```python
import jax
import jax.numpy as jnp
from jax import lax
from jax.experimental import pallas as pl
from jax.experimental.pallas import tpu as pltpu
from jax.sharding import PartitionSpec as P

bf16 = jnp.bfloat16
f32 = jnp.float32
learn_rate = 0.1

SLOTS = 4
HOT = 4
LOOK = 16
SHARDS = 32
CAP = 128
BATCHES = 2
GRAD_ROWS = BATCHES * CAP
TERM_ROWS = 128
ID_ROWS = 16
SENT_ROWS = GRAD_ROWS + TERM_ROWS + ID_ROWS

FIRST = [[x * 8 + y * 2 for x in range(4)] for y in range(4)] + [
    [x * 8 + y * 2 + 1 for y in range(4)] for x in range(4)
]
SECOND = [[x * 8 + y * 2 for y in range(4)] for x in range(4)] + [
    [x * 8 + y * 2 + 1 for x in range(4)] for y in range(4)
]
SWAP = [(i, i ^ 1) for i in range(SHARDS)]
NEAR = [[4 * i + j for j in range(4)] for i in range(4)]
FAR = [[4 * i + j for i in range(4)] for j in range(4)]


def exchange(value, axis, groups=None):
    return lax.all_to_all(
        value, axis, split_axis=0, concat_axis=0, tiled=True, axis_index_groups=groups
    )


def spread(value, axis, groups):
    return exchange(jnp.broadcast_to(value[None], (4,) + value.shape), axis, groups)


def dot(a, b, dims):
    return lax.dot_general(a, b, (dims, ((), ())), preferred_element_type=f32)


def column(row):
    return jnp.transpose(jnp.broadcast_to(row, (128, 128)))[:, 0:1]


def main_kernel(
    index_ref,
    place_ref,
    order_ref,
    own_ref,
    other_ref,
    label_ref,
    w_input_ref,
    w_hidden_hbm,
    w_output_ref,
    ids_ref,
    kept_ref,
    sent_ref,
    logit_ref,
    w_hidden_ref,
    table_ref,
    pooled_ref,
    slot_ref,
    turn_ref,
    pool_ref,
    act_ref,
    one_ref,
    two_ref,
    turned_ref,
    back_ref,
    term_ref,
    weight_sem,
):
    half = own_ref.shape[0]
    samples = pooled_ref.shape[0] // SLOTS
    fetch = pltpu.make_async_copy(w_hidden_hbm, w_hidden_ref, weight_sem)
    fetch.start()

    def widen(step, carry):
        at = pl.multiple_of(step * 256, 256)
        table_ref[pl.ds(at, 256), :] = own_ref[pl.ds(at, 256), :].astype(f32)
        table_ref[pl.ds(half + at, 256), :] = other_ref[pl.ds(at, 256), :].astype(f32)
        return carry

    lax.fori_loop(0, half // 256, widen, 0)

    def look(sample):
        for slot in range(SLOTS):
            first = sample * LOOK + slot * HOT
            total = table_ref[pl.ds(index_ref[first], 1), :]
            for hot in range(1, HOT):
                total = total + table_ref[pl.ds(index_ref[first + hot], 1), :]
            pooled_ref[pl.ds(slot * samples + sample, 1), :] = total

    def put(sample):
        for slot in range(SLOTS):
            first = sample * LOOK + slot * HOT
            row = pooled_ref[pl.ds(slot * samples + sample, 1), :]
            for hot in range(HOT):
                slot_ref[pl.ds(place_ref[first + hot], 1), :] = row

    def first_look(step, carry):
        slot_ref[pl.ds(pl.multiple_of(step * 1024, 1024), 1024), :] = jnp.zeros((1024, 128), f32)
        for turn in range(16):
            look(step * 16 + turn)
        return carry

    lax.fori_loop(0, 8, first_look, 0)

    features = SLOTS * 128

    def dense(b, work, start):
        rows = slice(b * 128, (b + 1) * 128)
        for slot in range(SLOTS):
            block = pooled_ref[slot * samples + b * 128 : slot * samples + (b + 1) * 128, :]
            turn_ref[slot * 128 : (slot + 1) * 128, :] = jnp.transpose(block)
            pool_ref[:, slot * 128 : (slot + 1) * 128] = block.astype(bf16)
        turned_ref[:, rows] = jnp.concatenate(
            [turn_ref[pl.ds(s, 16, stride=SHARDS), :] for s in range(SHARDS)], axis=0
        ).astype(bf16)

        def one(c, carry):
            cols = pl.ds(pl.multiple_of(c * 1024, 1024), 1024)
            pre = dot(pool_ref[...], w_input_ref[:, cols], ((1,), (0,)))
            one_ref[c] = pre
            act_ref[:, cols] = jnp.maximum(pre, 0.0).astype(bf16)
            for turn in range(32):
                work(start + c * 32 + turn)
            return carry

        lax.fori_loop(0, 1, one, 0)

        def two(c, carry):
            cols = pl.ds(pl.multiple_of(c * 1024, 1024), 1024)
            pre = dot(act_ref[...], w_hidden_ref[:, cols], ((1,), (0,)))
            two_ref[c] = pre
            act = jnp.maximum(pre, 0.0).astype(bf16).astype(f32)
            part = act * w_output_ref[:, cols].astype(f32)
            for turn in range(48):
                work(start + 32 + c * 48 + turn)
            return carry + part

        part = lax.fori_loop(0, 1, two, jnp.zeros((128, 1024), f32))
        logits = jnp.sum(part, axis=1, keepdims=True)
        logit_ref[b : b + 1, :] = jnp.transpose(jnp.broadcast_to(logits, (128, 128)))[0:1, :]
        slope = jax.nn.sigmoid(logits) - column(label_ref[b : b + 1, :])
        for c in range(1):
            cols = slice(c * 1024, (c + 1) * 1024)
            act_ref[:, cols] = jnp.where(
                two_ref[c] > 0, slope * w_output_ref[:, cols].astype(f32), 0.0
            ).astype(bf16)

        def back(c, carry):
            lines = pl.ds(pl.multiple_of(c * 1024, 1024), 1024)
            grad = dot(act_ref[...], w_hidden_ref[lines, :], ((1,), (1,)))
            grad = jnp.where(one_ref[c] > 0, grad, 0.0).astype(bf16)
            for h in range(8):
                back_ref[8 * c + h, rows, :] = grad[:, h * 128 : (h + 1) * 128]
            for turn in range(48):
                work(start + 80 + c * 48 + turn)
            return carry

        lax.fori_loop(0, 1, back, 0)
        back_one = jnp.concatenate([back_ref[j, rows, :] for j in range(8)], axis=1)
        back_in = dot(back_one, w_input_ref[...], ((1,), (1,))).astype(bf16).astype(f32)
        for slot in range(SLOTS):
            pooled_ref[slot * samples + b * 128 : slot * samples + (b + 1) * 128, :] = back_in[
                :, slot * 128 : (slot + 1) * 128
            ]

    fetch.wait()
    dense(0, look, 128)
    dense(1, put, 0)

    def last_put(step, carry):
        term_ref[step] = dot(turned_ref[...], back_ref[step], ((1,), (0,)))
        for turn in range(16):
            put(128 + step * 16 + turn)
        return carry

    lax.fori_loop(0, 8, last_put, 0)

    for target, base in ((sent_ref, SHARDS // 2), (kept_ref, 0)):

        def pack(owner, carry):
            at = pl.multiple_of((base + owner) * GRAD_ROWS, GRAD_ROWS)
            target[owner, 0:GRAD_ROWS, :] = slot_ref[pl.ds(at, GRAD_ROWS), :].astype(bf16)
            piece = pl.ds(pl.multiple_of(order_ref[base + owner] * 16, 16), 16)
            for j in range(8):
                target[owner, GRAD_ROWS + j * 16 : GRAD_ROWS + (j + 1) * 16, :] = term_ref[
                    j, piece, :
                ].astype(bf16)
            target[owner, GRAD_ROWS + TERM_ROWS : SENT_ROWS, :] = ids_ref[base + owner]
            return carry

        lax.fori_loop(0, SHARDS // 2, pack, 0, unroll=4)


def run_main(index, place, order, own, other, labels, w_input, w_hidden, w_output, ids):
    width = own.shape[1]
    samples = index.shape[0] // LOOK
    smem = pl.BlockSpec(memory_space=pltpu.SMEM)
    vmem = pl.BlockSpec(memory_space=pltpu.VMEM)
    return pl.pallas_call(
        main_kernel,
        out_shape=(
            jax.ShapeDtypeStruct((SHARDS // 2, SENT_ROWS, width), bf16),
            jax.ShapeDtypeStruct((SHARDS // 2, SENT_ROWS, width), bf16),
            jax.ShapeDtypeStruct((BATCHES, samples // BATCHES), f32),
        ),
        in_specs=[smem] * 3 + [vmem] * 4 + [pl.BlockSpec(memory_space=pl.ANY)] + [vmem] * 2,
        out_specs=(vmem, vmem, vmem),
        scratch_shapes=[
            pltpu.VMEM(w_hidden.shape, bf16),
            pltpu.VMEM((2 * own.shape[0], width), f32),
            pltpu.VMEM((samples * SLOTS, width), f32),
            pltpu.VMEM((SHARDS * GRAD_ROWS, width), f32),
            pltpu.VMEM((SLOTS * width, 128), f32),
            pltpu.VMEM((128, SLOTS * width), bf16),
            pltpu.VMEM((128, 1024), bf16),
            pltpu.VMEM((1, 128, 1024), f32),
            pltpu.VMEM((1, 128, 1024), f32),
            pltpu.VMEM((SLOTS * width, samples), bf16),
            pltpu.VMEM((8, samples, width), bf16),
            pltpu.VMEM((8, SLOTS * width, width), f32),
            pltpu.SemaphoreType.DMA(()),
        ],
        compiler_params=pltpu.CompilerParams(vmem_limit_bytes=44 * 1024 * 1024),
        cost_estimate=pl.CostEstimate(
            flops=2_000_000_000, bytes_accessed=12_000_000, transcendentals=256
        ),
    )(index, place, order, own, other, labels, w_input, w_hidden, w_output, ids)


def row_code(row):
    return jnp.where(row < 256, row + 1, 255 - row).astype(f32).astype(bf16)


def add_source(source, owner, total, term):
    rows = lax.broadcasted_iota(jnp.int32, (total.shape[0], CAP), 0)
    names = row_code(rows)
    coded = source[owner, GRAD_ROWS + TERM_ROWS : SENT_ROWS, :]
    one, zero = jnp.ones((), bf16), jnp.zeros((), bf16)
    pick = jnp.concatenate(
        [jnp.where(names == coded[b : b + 1], one, zero) for b in range(BATCHES)], axis=1
    )
    total = total + dot(pick, source[owner, 0:GRAD_ROWS, :], ((1,), (0,)))
    return total, term + source[owner, GRAD_ROWS : GRAD_ROWS + TERM_ROWS, :].astype(f32)


def kept_kernel(kept_ref, out_ref):
    rows = out_ref.shape[1] - TERM_ROWS
    width = out_ref.shape[2]

    def step(owner, carry):
        total = jnp.zeros((rows, width), f32)
        term = jnp.zeros((TERM_ROWS, width), f32)
        total, term = add_source(kept_ref, owner, total, term)
        out_ref[owner, 0:rows, :] = total.astype(bf16)
        out_ref[owner, rows : rows + TERM_ROWS, :] = term.astype(bf16)
        return carry

    lax.fori_loop(0, out_ref.shape[0], step, 0, unroll=8)


def got_kernel(base_ref, got_ref, out_ref):
    rows = out_ref.shape[1] - TERM_ROWS

    def step(owner, carry):
        total = base_ref[owner, 0:rows, :].astype(f32)
        term = base_ref[owner, rows : rows + TERM_ROWS, :].astype(f32)
        total, term = add_source(got_ref, owner, total, term)
        out_ref[owner, 0:rows, :] = total.astype(bf16)
        out_ref[owner, rows : rows + TERM_ROWS, :] = term.astype(bf16)
        return carry

    lax.fori_loop(0, out_ref.shape[0], step, 0, unroll=8)


def run_owner(kernel, rows, *operands):
    owners, _, width = operands[0].shape
    vmem = pl.BlockSpec(memory_space=pltpu.VMEM)
    return pl.pallas_call(
        kernel,
        out_shape=jax.ShapeDtypeStruct((owners, rows + TERM_ROWS, width), bf16),
        in_specs=[vmem] * len(operands),
        out_specs=vmem,
        compiler_params=pltpu.CompilerParams(vmem_limit_bytes=32 * 1024 * 1024),
        cost_estimate=pl.CostEstimate(
            flops=550_000_000, bytes_accessed=5_000_000, transcendentals=0
        ),
    )(*operands)


def near_kernel(got_ref, out_ref, term_ref):
    rows = got_ref.shape[1] - TERM_ROWS
    part = rows // 4
    for k in range(4):
        total = got_ref[0, k * part : (k + 1) * part, :].astype(f32)
        for source in range(1, 4):
            total = total + got_ref[source, k * part : (k + 1) * part, :].astype(f32)
        out_ref[k, 0:part, :] = total.astype(bf16)
    term = got_ref[0, rows : rows + TERM_ROWS, :].astype(f32)
    for source in range(1, 4):
        term = term + got_ref[source, rows : rows + TERM_ROWS, :].astype(f32)
    term_ref[...] = term
    for k in range(4):
        out_ref[k, part : part + 32, :] = term_ref[pl.ds(k, 32, stride=4), :].astype(bf16)


def run_near(got, rows):
    width = got.shape[2]
    vmem = pl.BlockSpec(memory_space=pltpu.VMEM)
    return pl.pallas_call(
        near_kernel,
        out_shape=jax.ShapeDtypeStruct((4, rows // 4 + 32, width), bf16),
        in_specs=[vmem],
        out_specs=vmem,
        scratch_shapes=[pltpu.VMEM((TERM_ROWS, width), f32)],
        compiler_params=pltpu.CompilerParams(vmem_limit_bytes=32 * 1024 * 1024),
        cost_estimate=pl.CostEstimate(flops=500_000, bytes_accessed=900_000, transcendentals=0),
    )(got)


def sum_of(got_ref, first, last):
    total = got_ref[0, first:last].astype(f32)
    for source in range(1, 4):
        total = total + got_ref[source, first:last].astype(f32)
    return total


def far_kernel(got_ref, out_ref):
    total = sum_of(got_ref, 0, out_ref.shape[1]).astype(bf16)
    for k in range(4):
        out_ref[k] = total


def run_far(got):
    _, rows, width = got.shape
    vmem = pl.BlockSpec(memory_space=pltpu.VMEM)
    return pl.pallas_call(
        far_kernel,
        out_shape=jax.ShapeDtypeStruct((4, rows - 8, width), bf16),
        in_specs=[vmem],
        out_specs=vmem,
        compiler_params=pltpu.CompilerParams(vmem_limit_bytes=16 * 1024 * 1024),
        cost_estimate=pl.CostEstimate(flops=70_000, bytes_accessed=300_000, transcendentals=0),
    )(got)


def final_kernel(total_ref, table_ref, sums_ref, got_ref, new_ref, term_ref):
    grad = total_ref[...].astype(f32)
    new_sums = sums_ref[...] + grad * grad
    new_ref[...] = table_ref[...] - learn_rate * grad / jnp.sqrt(new_sums)
    term_ref[...] = sum_of(got_ref, got_ref.shape[1] - 8, got_ref.shape[1])


def run_final(total, table, sums, got):
    vmem = pl.BlockSpec(memory_space=pltpu.VMEM)
    return pl.pallas_call(
        final_kernel,
        out_shape=(
            jax.ShapeDtypeStruct(table.shape, f32),
            jax.ShapeDtypeStruct((8, table.shape[1]), f32),
        ),
        in_specs=[vmem] * 4,
        out_specs=(vmem, vmem),
        compiler_params=pltpu.CompilerParams(vmem_limit_bytes=16 * 1024 * 1024),
        cost_estimate=pl.CostEstimate(
            flops=500_000, bytes_accessed=1_000_000, transcendentals=65536
        ),
    )(total, table, sums, got)


def owner_order(core):
    group = jnp.arange(SHARDS, dtype=jnp.int32)
    c = (group >> 4) ^ core
    slow, fast = (group >> 2) & 3, group & 3
    x, y = jnp.where(c == 0, slow, fast), jnp.where(c == 0, fast, slow)
    return x * 8 + y * 2 + c


def group_of(owner, core):
    x, y, c = owner >> 3, (owner >> 1) & 3, owner & 1
    return (c ^ core) * 16 + jnp.where(c == 0, x * 4 + y, y * 4 + x)


def plan_slots(owner, row, after):
    batches, samples, looks = owner.shape
    names, steps, turn, batch, spots, after = lax.optimization_barrier(
        (
            jnp.arange(SHARDS, dtype=jnp.int32),
            jnp.arange(samples),
            jnp.arange(looks),
            jnp.arange(batches, dtype=jnp.int32),
            jnp.arange(CAP, dtype=jnp.int32),
            after,
        )
    )
    hit = (owner[..., None] == names).astype(bf16).reshape(batches, samples, looks * SHARDS)
    before = (steps[None, :] < steps[:, None]).astype(bf16)
    rank = jnp.einsum("ts,bsn->btn", before, hit, preferred_element_type=f32)
    counts = jnp.sum(hit.astype(f32), axis=1).reshape(batches, looks, SHARDS)
    base = jnp.sum(
        jnp.where((turn[None, :] < turn[:, None])[None, :, :, None], counts[:, None], 0.0), axis=2
    ).reshape(batches, 1, looks * SHARDS)
    spot = jnp.sum(
        (hit.astype(f32) * (rank + base)).reshape(batches, samples, looks, SHARDS), axis=3
    ).astype(jnp.int32)
    place = owner * GRAD_ROWS + batch[:, None, None] * CAP + spot
    flat_hit = hit.reshape(batches, samples * looks, SHARDS)
    coded = flat_hit * row_code(row).reshape(batches, -1, 1)
    where = (spot.reshape(batches, -1, 1) == spots).astype(bf16)
    ids = jnp.einsum("bin,bip->bnp", coded, where, preferred_element_type=f32).astype(bf16)
    ids = jnp.pad(ids.transpose(1, 0, 2), ((0, 0), (0, ID_ROWS - batches), (0, 0)))
    return place.reshape(-1), ids


def table_index(owner, row, rows, core):
    x, y, c = owner >> 3, (owner >> 1) & 3, owner & 1
    chip = jnp.where(c == 0, y * 4 + x, x * 4 + y)
    return (((c ^ core) * 16 + chip) * rows + row).reshape(-1)


def local(
    owner_shard, local_row, click_label, row_table, squared_sums, w_input, w_hidden, w_output
):
    rows, width = row_table.shape
    owner = owner_shard[..., 0]
    core = lax.axis_index("shard") & 1
    table_low, core = lax.optimization_barrier((row_table.astype(bf16), core))
    line = spread(table_low, "shard", FIRST).reshape(4 * rows, width)
    own = spread(line, "shard", SECOND).reshape(16 * rows, width)
    own, owner, local_row, click_label, core = lax.optimization_barrier(
        (own, owner, local_row, click_label, core)
    )
    other = lax.ppermute(own, "shard", SWAP)
    index = table_index(owner, local_row, rows, core)
    order = owner_order(core)
    place, ids = plan_slots(group_of(owner, core), local_row, own)
    labels = click_label.astype(f32)
    kept, sent, logits = run_main(
        index,
        place,
        order,
        own,
        other,
        labels,
        w_input,
        w_hidden,
        w_output.reshape(1, -1),
        ids,
    )
    got = lax.ppermute(sent, "shard", SWAP)
    dense = run_owner(got_kernel, rows, run_owner(kept_kernel, rows, kept), got)
    dense = dense.reshape(4, 4 * (rows + TERM_ROWS), width)
    line = exchange(dense, "shard", FIRST).astype(f32)
    line = jnp.sum(line, axis=0).astype(bf16).reshape(4, rows + TERM_ROWS, width)
    near = exchange(run_near(exchange(line, "shard", SECOND), rows), "grp", NEAR).astype(f32)
    grads = jnp.sum(near[:, 0:128], axis=0).astype(bf16)
    term = jnp.sum(near[:, 128:160], axis=0)
    term = term.reshape(8, 4, width).transpose(1, 0, 2).astype(bf16)
    far = jnp.concatenate([jnp.broadcast_to(grads[None], (4, 128, width)), term], axis=1)
    far = exchange(far, "grp", FAR)
    total = exchange(run_far(far), "grp", NEAR).reshape(rows, width)
    new_table, input_grad = run_final(total, row_table, squared_sums, far)
    return (new_table, logits, input_grad.reshape(-1))


def solution(mesh):
    in_specs = (
        P(None, ("grp", "shard"), None, None),
        P(None, ("grp", "shard"), None),
        P(None, ("grp", "shard")),
        P("shard", None),
        P("shard", None),
        P(),
        P(),
        P(),
    )
    out_specs = (P("shard", None), P(None, ("grp", "shard")), P(("grp", "shard")))
    return jax.shard_map(local, mesh=mesh, in_specs=in_specs, out_specs=out_specs, check_vma=False)
```

```python
import jax
import jax.numpy as jnp
from jax import lax
from jax.experimental import pallas as pl
from jax.experimental.pallas import tpu as pltpu
from jax.sharding import PartitionSpec as P

bf16 = jnp.bfloat16
f32 = jnp.float32
learn_rate = 0.1

SLOTS = 4
HOT = 4
LOOK = 16
SHARDS = 32
CAP = 128
BATCHES = 2
GRAD_ROWS = BATCHES * CAP
TERM_ROWS = 128
ID_ROWS = 16
SENT_ROWS = GRAD_ROWS + TERM_ROWS + ID_ROWS

FIRST = [[x * 8 + y * 2 for x in range(4)] for y in range(4)] + [
    [x * 8 + y * 2 + 1 for y in range(4)] for x in range(4)
]
SECOND = [[x * 8 + y * 2 for y in range(4)] for x in range(4)] + [
    [x * 8 + y * 2 + 1 for x in range(4)] for y in range(4)
]
SWAP = [(i, i ^ 1) for i in range(SHARDS)]
NEAR = [[4 * i + j for j in range(4)] for i in range(4)]
FAR = [[4 * i + j for i in range(4)] for j in range(4)]


def exchange(value, axis, groups=None):
    return lax.all_to_all(
        value, axis, split_axis=0, concat_axis=0, tiled=True, axis_index_groups=groups
    )


def spread(value, axis, groups):
    return exchange(jnp.broadcast_to(value[None], (4,) + value.shape), axis, groups)


def dot(a, b, dims):
    return lax.dot_general(a, b, (dims, ((), ())), preferred_element_type=f32)


def column(row):
    return jnp.transpose(jnp.broadcast_to(row, (128, 128)))[:, 0:1]


def main_kernel(
    index_ref,
    place_ref,
    order_ref,
    own_ref,
    other_ref,
    label_ref,
    w_input_ref,
    w_hidden_hbm,
    w_output_ref,
    ids_ref,
    kept_ref,
    sent_ref,
    logit_ref,
    w_hidden_ref,
    table_ref,
    pooled_ref,
    slot_ref,
    turn_ref,
    pool_ref,
    act_ref,
    one_ref,
    two_ref,
    turned_ref,
    back_ref,
    term_ref,
    weight_sem,
):
    half = own_ref.shape[0]
    samples = pooled_ref.shape[0] // SLOTS
    fetch = pltpu.make_async_copy(w_hidden_hbm, w_hidden_ref, weight_sem)
    fetch.start()

    def widen(step, carry):
        at = pl.multiple_of(step * 256, 256)
        table_ref[pl.ds(at, 256), :] = own_ref[pl.ds(at, 256), :].astype(f32)
        table_ref[pl.ds(half + at, 256), :] = other_ref[pl.ds(at, 256), :].astype(f32)
        return carry

    lax.fori_loop(0, half // 256, widen, 0, unroll=4)

    def look(sample):
        for slot in range(SLOTS):
            first = sample * LOOK + slot * HOT
            total = table_ref[pl.ds(index_ref[first], 1), :]
            for hot in range(1, HOT):
                total = total + table_ref[pl.ds(index_ref[first + hot], 1), :]
            pooled_ref[pl.ds(slot * samples + sample, 1), :] = total

    def put(sample):
        for slot in range(SLOTS):
            first = sample * LOOK + slot * HOT
            row = pooled_ref[pl.ds(slot * samples + sample, 1), :]
            for hot in range(HOT):
                slot_ref[pl.ds(place_ref[first + hot], 1), :] = row

    def first_look(step, carry):
        slot_ref[pl.ds(pl.multiple_of(step * 1024, 1024), 1024), :] = jnp.zeros((1024, 128), f32)
        for turn in range(16):
            look(step * 16 + turn)
        return carry

    lax.fori_loop(0, 8, first_look, 0, unroll=2)

    features = SLOTS * 128

    def dense(b, work, start):
        rows = slice(b * 128, (b + 1) * 128)
        for slot in range(SLOTS):
            block = pooled_ref[slot * samples + b * 128 : slot * samples + (b + 1) * 128, :]
            turn_ref[slot * 128 : (slot + 1) * 128, :] = jnp.transpose(block)
            pool_ref[:, slot * 128 : (slot + 1) * 128] = block.astype(bf16)
        turned_ref[:, rows] = jnp.concatenate(
            [turn_ref[pl.ds(s, 16, stride=SHARDS), :] for s in range(SHARDS)], axis=0
        ).astype(bf16)

        def one(c, carry):
            cols = pl.ds(pl.multiple_of(c * 1024, 1024), 1024)
            pre = dot(pool_ref[...], w_input_ref[:, cols], ((1,), (0,)))
            one_ref[c] = pre
            act_ref[:, cols] = jnp.maximum(pre, 0.0).astype(bf16)
            for turn in range(32):
                work(start + c * 32 + turn)
            return carry

        lax.fori_loop(0, 1, one, 0)

        def two(c, carry):
            cols = pl.ds(pl.multiple_of(c * 1024, 1024), 1024)
            pre = dot(act_ref[...], w_hidden_ref[:, cols], ((1,), (0,)))
            two_ref[c] = pre
            act = jnp.maximum(pre, 0.0).astype(bf16).astype(f32)
            part = act * w_output_ref[:, cols].astype(f32)
            for turn in range(48):
                work(start + 32 + c * 48 + turn)
            return carry + part

        part = lax.fori_loop(0, 1, two, jnp.zeros((128, 1024), f32))
        logits = jnp.sum(part, axis=1, keepdims=True)
        logit_ref[b : b + 1, :] = jnp.transpose(jnp.broadcast_to(logits, (128, 128)))[0:1, :]
        slope = jax.nn.sigmoid(logits) - column(label_ref[b : b + 1, :])
        for c in range(1):
            cols = slice(c * 1024, (c + 1) * 1024)
            act_ref[:, cols] = jnp.where(
                two_ref[c] > 0, slope * w_output_ref[:, cols].astype(f32), 0.0
            ).astype(bf16)

        def back(c, carry):
            lines = pl.ds(pl.multiple_of(c * 1024, 1024), 1024)
            grad = dot(act_ref[...], w_hidden_ref[lines, :], ((1,), (1,)))
            grad = jnp.where(one_ref[c] > 0, grad, 0.0).astype(bf16)
            for h in range(8):
                back_ref[8 * c + h, rows, :] = grad[:, h * 128 : (h + 1) * 128]
            for turn in range(48):
                work(start + 80 + c * 48 + turn)
            return carry

        lax.fori_loop(0, 1, back, 0)
        back_one = jnp.concatenate([back_ref[j, rows, :] for j in range(8)], axis=1)
        back_in = dot(back_one, w_input_ref[...], ((1,), (1,))).astype(bf16).astype(f32)
        for slot in range(SLOTS):
            pooled_ref[slot * samples + b * 128 : slot * samples + (b + 1) * 128, :] = back_in[
                :, slot * 128 : (slot + 1) * 128
            ]

    fetch.wait()
    dense(0, look, 128)
    dense(1, put, 0)

    def last_put(step, carry):
        term_ref[step] = dot(turned_ref[...], back_ref[step], ((1,), (0,)))
        for turn in range(16):
            put(128 + step * 16 + turn)
        return carry

    lax.fori_loop(0, 8, last_put, 0, unroll=2)

    for target, base in ((sent_ref, SHARDS // 2), (kept_ref, 0)):

        def pack(owner, carry):
            at = pl.multiple_of((base + owner) * GRAD_ROWS, GRAD_ROWS)
            target[owner, 0:GRAD_ROWS, :] = slot_ref[pl.ds(at, GRAD_ROWS), :].astype(bf16)
            piece = pl.ds(pl.multiple_of(order_ref[base + owner] * 16, 16), 16)
            for j in range(8):
                target[owner, GRAD_ROWS + j * 16 : GRAD_ROWS + (j + 1) * 16, :] = term_ref[
                    j, piece, :
                ].astype(bf16)
            target[owner, GRAD_ROWS + TERM_ROWS : SENT_ROWS, :] = ids_ref[base + owner]
            return carry

        lax.fori_loop(0, SHARDS // 2, pack, 0, unroll=16)


def run_main(index, place, order, own, other, labels, w_input, w_hidden, w_output, ids):
    width = own.shape[1]
    samples = index.shape[0] // LOOK
    smem = pl.BlockSpec(memory_space=pltpu.SMEM)
    vmem = pl.BlockSpec(memory_space=pltpu.VMEM)
    return pl.pallas_call(
        main_kernel,
        out_shape=(
            jax.ShapeDtypeStruct((SHARDS // 2, SENT_ROWS, width), bf16),
            jax.ShapeDtypeStruct((SHARDS // 2, SENT_ROWS, width), bf16),
            jax.ShapeDtypeStruct((BATCHES, samples // BATCHES), f32),
        ),
        in_specs=[smem] * 3 + [vmem] * 4 + [pl.BlockSpec(memory_space=pl.ANY)] + [vmem] * 2,
        out_specs=(vmem, vmem, vmem),
        scratch_shapes=[
            pltpu.VMEM(w_hidden.shape, bf16),
            pltpu.VMEM((2 * own.shape[0], width), f32),
            pltpu.VMEM((samples * SLOTS, width), f32),
            pltpu.VMEM((SHARDS * GRAD_ROWS, width), f32),
            pltpu.VMEM((SLOTS * width, 128), f32),
            pltpu.VMEM((128, SLOTS * width), bf16),
            pltpu.VMEM((128, 1024), bf16),
            pltpu.VMEM((1, 128, 1024), f32),
            pltpu.VMEM((1, 128, 1024), f32),
            pltpu.VMEM((SLOTS * width, samples), bf16),
            pltpu.VMEM((8, samples, width), bf16),
            pltpu.VMEM((8, SLOTS * width, width), f32),
            pltpu.SemaphoreType.DMA(()),
        ],
        compiler_params=pltpu.CompilerParams(vmem_limit_bytes=44 * 1024 * 1024),
        cost_estimate=pl.CostEstimate(
            flops=2_000_000_000, bytes_accessed=12_000_000, transcendentals=256
        ),
    )(index, place, order, own, other, labels, w_input, w_hidden, w_output, ids)


def row_code(row):
    return jnp.where(row < 256, row + 1, 255 - row).astype(f32).astype(bf16)


def add_source(source, owner, total, term):
    rows = lax.broadcasted_iota(jnp.int32, (total.shape[0], CAP), 0)
    names = row_code(rows)
    coded = source[owner, GRAD_ROWS + TERM_ROWS : SENT_ROWS, :]
    one, zero = jnp.ones((), bf16), jnp.zeros((), bf16)
    pick = jnp.concatenate(
        [jnp.where(names == coded[b : b + 1], one, zero) for b in range(BATCHES)], axis=1
    )
    total = total + dot(pick, source[owner, 0:GRAD_ROWS, :], ((1,), (0,)))
    return total, term + source[owner, GRAD_ROWS : GRAD_ROWS + TERM_ROWS, :].astype(f32)


def kept_kernel(kept_ref, out_ref):
    rows = out_ref.shape[1] - TERM_ROWS
    width = out_ref.shape[2]

    def step(owner, carry):
        total = jnp.zeros((rows, width), f32)
        term = jnp.zeros((TERM_ROWS, width), f32)
        total, term = add_source(kept_ref, owner, total, term)
        out_ref[owner, 0:rows, :] = total.astype(bf16)
        out_ref[owner, rows : rows + TERM_ROWS, :] = term.astype(bf16)
        return carry

    lax.fori_loop(0, out_ref.shape[0], step, 0, unroll=8)


def got_kernel(base_ref, got_ref, out_ref):
    rows = out_ref.shape[1] - TERM_ROWS

    def step(owner, carry):
        total = base_ref[owner, 0:rows, :].astype(f32)
        term = base_ref[owner, rows : rows + TERM_ROWS, :].astype(f32)
        total, term = add_source(got_ref, owner, total, term)
        out_ref[owner, 0:rows, :] = total.astype(bf16)
        out_ref[owner, rows : rows + TERM_ROWS, :] = term.astype(bf16)
        return carry

    lax.fori_loop(0, out_ref.shape[0], step, 0, unroll=8)


def run_owner(kernel, rows, *operands):
    owners, _, width = operands[0].shape
    vmem = pl.BlockSpec(memory_space=pltpu.VMEM)
    return pl.pallas_call(
        kernel,
        out_shape=jax.ShapeDtypeStruct((owners, rows + TERM_ROWS, width), bf16),
        in_specs=[vmem] * len(operands),
        out_specs=vmem,
        compiler_params=pltpu.CompilerParams(vmem_limit_bytes=32 * 1024 * 1024),
        cost_estimate=pl.CostEstimate(
            flops=550_000_000, bytes_accessed=5_000_000, transcendentals=0
        ),
    )(*operands)


def near_kernel(got_ref, out_ref, term_ref):
    rows = got_ref.shape[1] - TERM_ROWS
    part = rows // 4
    for k in range(4):
        total = got_ref[0, k * part : (k + 1) * part, :].astype(f32)
        for source in range(1, 4):
            total = total + got_ref[source, k * part : (k + 1) * part, :].astype(f32)
        out_ref[k, 0:part, :] = total.astype(bf16)
    term = got_ref[0, rows : rows + TERM_ROWS, :].astype(f32)
    for source in range(1, 4):
        term = term + got_ref[source, rows : rows + TERM_ROWS, :].astype(f32)
    term_ref[...] = term
    for k in range(4):
        out_ref[k, part : part + 32, :] = term_ref[pl.ds(k, 32, stride=4), :].astype(bf16)


def run_near(got, rows):
    width = got.shape[2]
    vmem = pl.BlockSpec(memory_space=pltpu.VMEM)
    return pl.pallas_call(
        near_kernel,
        out_shape=jax.ShapeDtypeStruct((4, rows // 4 + 32, width), bf16),
        in_specs=[vmem],
        out_specs=vmem,
        scratch_shapes=[pltpu.VMEM((TERM_ROWS, width), f32)],
        compiler_params=pltpu.CompilerParams(vmem_limit_bytes=32 * 1024 * 1024),
        cost_estimate=pl.CostEstimate(flops=500_000, bytes_accessed=900_000, transcendentals=0),
    )(got)


def sum_of(got_ref, first, last):
    total = got_ref[0, first:last].astype(f32)
    for source in range(1, 4):
        total = total + got_ref[source, first:last].astype(f32)
    return total


def far_kernel(got_ref, out_ref):
    total = sum_of(got_ref, 0, out_ref.shape[1]).astype(bf16)
    for k in range(4):
        out_ref[k] = total


def run_far(got):
    _, rows, width = got.shape
    vmem = pl.BlockSpec(memory_space=pltpu.VMEM)
    return pl.pallas_call(
        far_kernel,
        out_shape=jax.ShapeDtypeStruct((4, rows - 8, width), bf16),
        in_specs=[vmem],
        out_specs=vmem,
        compiler_params=pltpu.CompilerParams(vmem_limit_bytes=16 * 1024 * 1024),
        cost_estimate=pl.CostEstimate(flops=70_000, bytes_accessed=300_000, transcendentals=0),
    )(got)


def final_kernel(total_ref, table_ref, sums_ref, got_ref, new_ref, term_ref):
    grad = total_ref[...].astype(f32)
    new_sums = sums_ref[...] + grad * grad
    new_ref[...] = table_ref[...] - learn_rate * grad / jnp.sqrt(new_sums)
    term_ref[...] = sum_of(got_ref, got_ref.shape[1] - 8, got_ref.shape[1])


def run_final(total, table, sums, got):
    vmem = pl.BlockSpec(memory_space=pltpu.VMEM)
    return pl.pallas_call(
        final_kernel,
        out_shape=(
            jax.ShapeDtypeStruct(table.shape, f32),
            jax.ShapeDtypeStruct((8, table.shape[1]), f32),
        ),
        in_specs=[vmem] * 4,
        out_specs=(vmem, vmem),
        compiler_params=pltpu.CompilerParams(vmem_limit_bytes=16 * 1024 * 1024),
        cost_estimate=pl.CostEstimate(
            flops=500_000, bytes_accessed=1_000_000, transcendentals=65536
        ),
    )(total, table, sums, got)


def owner_order(core):
    group = jnp.arange(SHARDS, dtype=jnp.int32)
    c = (group >> 4) ^ core
    slow, fast = (group >> 2) & 3, group & 3
    x, y = jnp.where(c == 0, slow, fast), jnp.where(c == 0, fast, slow)
    return x * 8 + y * 2 + c


def group_of(owner, core):
    x, y, c = owner >> 3, (owner >> 1) & 3, owner & 1
    return (c ^ core) * 16 + jnp.where(c == 0, x * 4 + y, y * 4 + x)


def plan_slots(owner, row, after):
    batches, samples, looks = owner.shape
    names, steps, turn, batch, spots, after = lax.optimization_barrier(
        (
            jnp.arange(SHARDS, dtype=jnp.int32),
            jnp.arange(samples),
            jnp.arange(looks),
            jnp.arange(batches, dtype=jnp.int32),
            jnp.arange(CAP, dtype=jnp.int32),
            after,
        )
    )
    hit = (owner[..., None] == names).astype(bf16).reshape(batches, samples, looks * SHARDS)
    before = (steps[None, :] < steps[:, None]).astype(bf16)
    rank = jnp.einsum("ts,bsn->btn", before, hit, preferred_element_type=f32)
    counts = jnp.sum(hit.astype(f32), axis=1).reshape(batches, looks, SHARDS)
    base = jnp.sum(
        jnp.where((turn[None, :] < turn[:, None])[None, :, :, None], counts[:, None], 0.0), axis=2
    ).reshape(batches, 1, looks * SHARDS)
    spot = jnp.sum(
        (hit.astype(f32) * (rank + base)).reshape(batches, samples, looks, SHARDS), axis=3
    ).astype(jnp.int32)
    place = owner * GRAD_ROWS + batch[:, None, None] * CAP + spot
    flat_hit = hit.reshape(batches, samples * looks, SHARDS)
    coded = flat_hit * row_code(row).reshape(batches, -1, 1)
    where = (spot.reshape(batches, -1, 1) == spots).astype(bf16)
    ids = jnp.einsum("bin,bip->bnp", coded, where, preferred_element_type=f32).astype(bf16)
    ids = jnp.pad(ids.transpose(1, 0, 2), ((0, 0), (0, ID_ROWS - batches), (0, 0)))
    return place.reshape(-1), ids


def table_index(owner, row, rows, core):
    x, y, c = owner >> 3, (owner >> 1) & 3, owner & 1
    chip = jnp.where(c == 0, y * 4 + x, x * 4 + y)
    return (((c ^ core) * 16 + chip) * rows + row).reshape(-1)


def local(
    owner_shard, local_row, click_label, row_table, squared_sums, w_input, w_hidden, w_output
):
    rows, width = row_table.shape
    owner = owner_shard[..., 0]
    core = lax.axis_index("shard") & 1
    table_low, core = lax.optimization_barrier((row_table.astype(bf16), core))
    line = spread(table_low, "shard", FIRST).reshape(4 * rows, width)
    own = spread(line, "shard", SECOND).reshape(16 * rows, width)
    own, owner, local_row, click_label, core = lax.optimization_barrier(
        (own, owner, local_row, click_label, core)
    )
    other = lax.ppermute(own, "shard", SWAP)
    index = table_index(owner, local_row, rows, core)
    order = owner_order(core)
    place, ids = plan_slots(group_of(owner, core), local_row, own)
    labels = click_label.astype(f32)
    kept, sent, logits = run_main(
        index,
        place,
        order,
        own,
        other,
        labels,
        w_input,
        w_hidden,
        w_output.reshape(1, -1),
        ids,
    )
    got = lax.ppermute(sent, "shard", SWAP)
    dense = run_owner(got_kernel, rows, run_owner(kept_kernel, rows, kept), got)
    dense = dense.reshape(4, 4 * (rows + TERM_ROWS), width)
    line = exchange(dense, "shard", FIRST).astype(f32)
    line = jnp.sum(line, axis=0).astype(bf16).reshape(4, rows + TERM_ROWS, width)
    near = exchange(run_near(exchange(line, "shard", SECOND), rows), "grp", NEAR).astype(f32)
    grads = jnp.sum(near[:, 0:128], axis=0).astype(bf16)
    term = jnp.sum(near[:, 128:160], axis=0)
    term = term.reshape(8, 4, width).transpose(1, 0, 2).astype(bf16)
    far = jnp.concatenate([jnp.broadcast_to(grads[None], (4, 128, width)), term], axis=1)
    far = exchange(far, "grp", FAR)
    total = exchange(run_far(far), "grp", NEAR).reshape(rows, width)
    new_table, input_grad = run_final(total, row_table, squared_sums, far)
    return (new_table, logits, input_grad.reshape(-1))


def solution(mesh):
    in_specs = (
        P(None, ("grp", "shard"), None, None),
        P(None, ("grp", "shard"), None),
        P(None, ("grp", "shard")),
        P("shard", None),
        P("shard", None),
        P(),
        P(),
        P(),
    )
    out_specs = (P("shard", None), P(None, ("grp", "shard")), P(("grp", "shard")))
    return jax.shard_map(local, mesh=mesh, in_specs=in_specs, out_specs=out_specs, check_vma=False)
```
